32 devices in a mesh: frame: 2 (over core), patch: 8 (over z, x), tp: 2 (over y).
Axes of the slice: x: 2, y: 2, z: 4, core: 2. Of those that a mesh axis runs over, the one named last changes fastest.
Arguments:
- residual_codes: int32 [4, 16, 32, 1536], P('frame', 'patch', None, 'tp'), may hold values from -127 to 127
- exponents: int32 [4, 16, 32, 24], P('frame', 'patch', None, 'tp'), may hold values from -8 to -4
- conv_weight: bfloat16 [3, 3, 3, 1536], replicated, may hold values from -1.25 to 1.25
- timestep: int32 [4], P('frame'), may hold values from 0 to 49
- modulation: bfloat16 [50, 2, 1536], replicated, may hold values from -3 to 3
- query_weight: bfloat16 [1536, 768], P(None, 'tp'), as said below
- key_weight: bfloat16 [1536, 768], P(None, 'tp'), as said below
- value_weight: bfloat16 [1536, 768], P(None, 'tp'), may hold values from -0.15625 to 0.15625
Outputs:
- attended: bfloat16 [4, 16, 32, 768], P('frame', 'patch', None, 'tp')
The draws below stay inside these ranges and needn't reach their ends.
Inputs may be any that keep to these rules, and one draw needn't show every extreme that they name: `query_weight`: entries of order D ** -0.5. `key_weight`: entries of order D ** -0.5.
All inputs are finite; a program needn't handle non-finite values.
Results may differ from the reference program's by a relative error of at most 0.02.
The reference program's roundings to bfloat16 on the way count: a program that leaves them out, or rounds other values in their place, can miss the bound.
Values may be sent and summed in bfloat16 or wider, within the bound.
A program may use at most 128 MiB of HBM per device.

```python
import math
import jax
import jax.numpy as jnp
from jax import lax

D = 1536
HEADS = 12
HEAD_DIM = 64
BLOCK = 64
STEPS = 50
F_DEV = 2
WW = 32
FR = 4
HH = 16
N_FRAME = 2


def projection(key):
    base = jax.random.normal(key, (D, HEADS * HEAD_DIM), jnp.float32) / math.sqrt(D)
    return base


def draw_query_weight(key, part):
    key = jax.random.fold_in(key, 11)
    matrix = projection(key)
    return matrix.astype(jnp.bfloat16)


def draw_key_weight(key, part):
    key = jax.random.fold_in(key, 23)
    matrix = projection(key)
    return matrix.astype(jnp.bfloat16)


def set_ends(values, key, least, top_value):
    shape = values.shape
    place = [jax.random.randint(jax.random.fold_in(key, axis), (), 0, shape[axis]) for axis in range(len(shape))]
    values = values.at[tuple(place)].set(least)
    longest = shape.index(max(shape))
    place[longest] = (place[longest] + 1) % shape[longest]
    return values.at[tuple(place)].set(top_value)


def level_of(own_key, dims, pieces, smallest, high):
    level, own = 1.0, jax.random.fold_in(own_key, 6)
    for position, blocks in pieces:
        steps = jnp.exp(jax.random.uniform(jax.random.fold_in(own, position), (blocks,), jnp.float32, smallest / len(pieces), high / len(pieces)))
        level = level * jnp.repeat(steps, dims[position] // blocks).reshape([-1 if axis == position else 1 for axis in range(len(dims))])
    return level


def centred(key, extent, width, limit, cuts=(), kind=jnp.bfloat16):
    entries = width * jax.random.normal(key, extent, jnp.float32)
    if cuts:
        entries = entries * level_of(key, extent, cuts, -0.22, 0.18)
    return jnp.clip(entries, -limit, limit).astype(kind)


def setup_inputs(seed: int = 0) -> dict:
    key_of = jax.random.split(jax.random.key(seed), 9)
    residual_codes = set_ends(jax.random.randint(key_of[0], (FR, HH, WW, D), -127, 128), jax.random.fold_in(key_of[0], 1), -127, 127).astype(jnp.int32)
    exponents = set_ends(jax.random.randint(key_of[1], (FR, HH, WW, D // BLOCK), -8, -3), jax.random.fold_in(key_of[1], 1), -8, (-3) - 1).astype(jnp.int32)
    conv_weight = centred(key_of[2], (3, 3, 3, D), 27 ** -0.5, 1.25)
    timestep = set_ends(jax.random.randint(key_of[3], (FR,), 0, STEPS), jax.random.fold_in(key_of[3], 1), 0, STEPS - 1).astype(jnp.int32)
    modulation = centred(key_of[4], (STEPS, 2, D), 0.5, 3.0)
    query_weight = draw_query_weight(jax.random.fold_in(key_of[8], 71), 0)
    key_weight = draw_key_weight(jax.random.fold_in(key_of[8], 71), 0)
    value_weight = centred(key_of[7], (D, HEADS * HEAD_DIM), D ** -0.5, 0.15625, ((1, 2),))
    return {"residual_codes": residual_codes, "exponents": exponents, "conv_weight": conv_weight, "timestep": timestep, "modulation": modulation, "query_weight": query_weight, "key_weight": key_weight, "value_weight": value_weight}


def dequantize(residual_codes, exponents):
    groups = exponents.shape[-1]
    model_width = residual_codes.shape[-1]
    factor = jnp.exp2(exponents.astype(jnp.float32))
    values = residual_codes.astype(jnp.float32).reshape(residual_codes.shape[:-1] + (groups, model_width // groups))
    return (values * factor[..., None]).reshape(residual_codes.shape)

def convolve(padded, kernel, out_shape):
    frames, tile_rows, tile_cols = out_shape
    result = jnp.zeros(out_shape + (kernel.shape[-1],), jnp.float32)
    for shift_f in range(3):
        for shift_h in range(3):
            for shift_w in range(3):
                window = padded[shift_f:shift_f + frames, shift_h:shift_h + tile_rows, shift_w:shift_w + tile_cols, :]
                result = result + window.astype(jnp.float32) * kernel[shift_f, shift_h, shift_w].astype(jnp.float32)
    return result

def modulate(mixed, modulation, timestep):
    selector = (jnp.arange(modulation.shape[0], dtype=jnp.int32)[None, :] == timestep[:, None]).astype(jnp.float32)
    picked = jnp.einsum('fs,sjd->fjd', selector, modulation.astype(jnp.float32))
    shift_rows = picked[:, 0][:, None, None, :]
    scale_rows = picked[:, 1][:, None, None, :]
    values = mixed.astype(jnp.float32)
    average = lax.optimization_barrier(jnp.mean(values, axis=-1, keepdims=True))
    centered = values - average
    variance = lax.optimization_barrier(jnp.mean(centered * centered, axis=-1, keepdims=True))
    normed = centered / jnp.sqrt(variance + 1e-06) * (1.0 + scale_rows) + shift_rows
    return normed.astype(jnp.bfloat16)

def reference(residual_codes, exponents, conv_weight, timestep, modulation, query_weight, key_weight, value_weight):
    inputs = dequantize(residual_codes, exponents)
    padded = jnp.pad(inputs.astype(jnp.bfloat16), ((1, 1), (1, 1), (1, 1), (0, 0)))
    mixed = (inputs + convolve(padded, conv_weight, (FR, HH, WW))).astype(jnp.bfloat16)
    normed = modulate(mixed, modulation, timestep).reshape(FR * HH * WW, D)
    queries = jnp.dot(normed, query_weight, preferred_element_type=jnp.float32).astype(jnp.bfloat16)
    key_rows = jnp.dot(normed, key_weight, preferred_element_type=jnp.float32).astype(jnp.bfloat16)
    value_rows = jnp.dot(normed, value_weight, preferred_element_type=jnp.float32).astype(jnp.bfloat16)
    stretch_len = F_DEV * HH * WW

    def heads_major(matrix):
        shaped = matrix.reshape(N_FRAME, stretch_len, HEADS, HEAD_DIM).transpose(0, 2, 1, 3)
        return shaped.reshape(N_FRAME * HEADS, stretch_len, HEAD_DIM)

    def attend(triple):
        query_part, key_part, value_part = triple
        scores = jnp.dot(query_part, key_part.T, preferred_element_type=jnp.float32) * HEAD_DIM ** (-0.5)
        row_max = lax.optimization_barrier(jnp.max(scores, axis=1, keepdims=True))
        exps = jnp.exp(scores - row_max)
        totals = lax.optimization_barrier(jnp.sum(exps, axis=1, keepdims=True))
        summed = jnp.dot(exps.astype(jnp.bfloat16), value_part, preferred_element_type=jnp.float32)
        return (summed / totals).astype(jnp.bfloat16)
    outputs = lax.map(attend, (heads_major(queries), heads_major(key_rows), heads_major(value_rows)))
    outputs = outputs.reshape(N_FRAME, HEADS, stretch_len, HEAD_DIM).transpose(0, 2, 1, 3)
    return outputs.reshape(FR, HH, WW, HEADS * HEAD_DIM)
```

```python
import functools

import jax
import jax.numpy as jnp
from jax import lax
from jax.experimental import pallas as pl
from jax.experimental.pallas import tpu as pltpu
from jax.sharding import PartitionSpec as P

HEAD_DIM = 64
LANES = 128
MESH = pl.DeviceIdType.MESH


def flip(index, mask):
    bit = 1
    while bit <= mask:
        if mask & bit:
            index = index + bit - 2 * bit * lax.rem(lax.div(index, bit), 2)
        bit *= 2
    return index


def kernel(
    sizes,
    ts_hbm,
    codes_hbm,
    exps_hbm,
    taps_hbm,
    mod_hbm,
    wq_hbm,
    wk_hbm,
    wv_hbm,
    out_ref,
    ts_ref,
    codes_ref,
    exps_ref,
    taps_ref,
    mod_ref,
    pad,
    taps,
    mixed,
    normed,
    wkv,
    wq,
    kv_own,
    kv_all,
    q_own,
    q_pack,
    q_peer,
    o_pack,
    o_peer,
    in_sem,
    row_send,
    row_recv,
    frame_send,
    frame_recv,
    corner_send,
    corner_recv,
    mix_send,
    mix_recv,
    a_send,
    a_recv,
    b_send,
    b_recv,
    c_send,
    c_recv,
    q_send,
    q_recv,
    o_send,
    o_recv,
):
    n_frame, n_patch, n_tp = sizes
    frames, rows, cols, channels = codes_ref.shape
    tokens = frames * rows * cols
    half = rows * cols
    local_width = wq_hbm.shape[1]
    local_heads = local_width // HEAD_DIM
    heads = local_heads // 2
    width = n_tp * channels
    f_me = lax.axis_index("frame")
    p_me = lax.axis_index("patch")
    t_me = lax.axis_index("tp")
    t_peer = 1 - t_me
    side = lax.rem(lax.div(p_me, 2), 2)
    lead = lax.rem(f_me, 2)
    order = (lead, 1 - lead)
    p_pair = flip(p_me, 2)
    p_twin = flip(p_me, 1)
    far = list(range(4, n_patch, 4))

    loads = [
        pltpu.make_async_copy(src, dst, in_sem.at[i])
        for i, (src, dst) in enumerate(
            [
                (codes_hbm, codes_ref),
                (exps_hbm, exps_ref),
                (taps_hbm, taps_ref),
                (ts_hbm, ts_ref),
                (mod_hbm, mod_ref),
                (wk_hbm, wkv.at[:, pl.ds(0, local_width)]),
                (wv_hbm, wkv.at[:, pl.ds(local_width, local_width)]),
                (wq_hbm, wq),
            ]
        )
    ]
    for copy in loads:
        copy.start()

    barrier = pltpu.get_barrier_semaphore()

    def signal(f, p, t):
        pl.semaphore_signal(barrier, inc=1, device_id=(f, p, t), device_id_type=MESH)

    f_there = {-1: f_me > 0, 1: f_me < n_frame - 1}
    p_there = {-1: p_me > 0, 1: p_me < n_patch - 1}
    count = 3 + 2 * len(far)
    for d in (-1, 1):

        @pl.when(f_there[d])
        def _():
            signal(f_me + d, p_me, t_me)

        @pl.when(p_there[d])
        def _():
            signal(f_me, p_me + d, t_me)

        count = count + f_there[d].astype(jnp.int32) + p_there[d].astype(jnp.int32)
    signal(f_me, p_me, t_peer)
    signal(f_me, p_pair, t_me)
    signal(f_me, p_twin, t_me)
    for k in far:
        signal(f_me, flip(p_me, k), t_me)
        signal(f_me, flip(p_me, k + 2), t_me)

    for d in (-1, 1):
        edge_f = 0 if d < 0 else frames + 1
        edge_r = 0 if d < 0 else rows + 1

        @pl.when(jnp.logical_not(f_there[d]))
        def _():
            pad[edge_f] = jnp.zeros((rows + 2, cols, channels), jnp.bfloat16)

        @pl.when(jnp.logical_not(p_there[d]))
        def _():
            pad[1 : 1 + frames, edge_r] = jnp.zeros((frames, cols, channels), jnp.bfloat16)
            for g in (-1, 1):

                @pl.when(f_there[g])
                def _():
                    pad[0 if g < 0 else frames + 1, edge_r] = jnp.zeros(
                        (cols, channels), jnp.bfloat16
                    )

    groups = exps_ref.shape[1]
    span = channels // groups
    spread = (
        lax.broadcasted_iota(jnp.int32, (groups, channels), 1) // span
        == lax.broadcasted_iota(jnp.int32, (groups, channels), 0)
    ).astype(jnp.float32).astype(jnp.bfloat16)
    loads[0].wait()
    loads[1].wait()
    for f in range(frames):
        for r in range(rows):
            factor = jnp.left_shift(jnp.ones((groups, cols), jnp.int32), exps_ref[f, :, r, :] + 8)
            factor = (factor.astype(jnp.float32) * (2.0**-8)).astype(jnp.bfloat16)
            factor = lax.dot_general(
                factor, spread, (((0,), (0,)), ((), ())), preferred_element_type=jnp.float32
            )
            values = codes_ref[f, r].astype(jnp.float32) * factor
            pad[f + 1, r + 1] = values.astype(jnp.bfloat16)

    pl.semaphore_wait(barrier, count)

    def row_copy(d, part):
        frame = 1 + order[1 - part]
        number = (0 if d < 0 else 2) + part
        return pltpu.make_async_remote_copy(
            src_ref=pad.at[frame, rows if d > 0 else 1],
            dst_ref=pad.at[frame, 0 if d > 0 else rows + 1],
            send_sem=row_send.at[number],
            recv_sem=row_recv.at[number],
            device_id=(f_me, p_me + d, t_me),
            device_id_type=MESH,
        )

    def frame_copy(d):
        number = 0 if d < 0 else 1
        return pltpu.make_async_remote_copy(
            src_ref=pad.at[frames if d > 0 else 1, pl.ds(1, rows)],
            dst_ref=pad.at[0 if d > 0 else frames + 1, pl.ds(1, rows)],
            send_sem=frame_send.at[number],
            recv_sem=frame_recv.at[number],
            device_id=(f_me + d, p_me, t_me),
            device_id_type=MESH,
        )

    def corner_copy(d, g):
        number = (0 if d < 0 else 2) + (0 if g < 0 else 1)
        row = 0 if g > 0 else rows + 1
        return pltpu.make_async_remote_copy(
            src_ref=pad.at[frames if d > 0 else 1, row],
            dst_ref=pad.at[0 if d > 0 else frames + 1, row],
            send_sem=corner_send.at[number],
            recv_sem=corner_recv.at[number],
            device_id=(f_me + d, p_me, t_me),
            device_id_type=MESH,
        )

    for part in range(2):
        for d in (-1, 1):
            pl.when(p_there[d])(row_copy(d, part).start)
    for d in (-1, 1):
        pl.when(f_there[d])(frame_copy(d).start)

    loads[2].wait()
    own_lanes = pl.ds(pl.multiple_of(t_me * channels, LANES), channels)
    for a in range(3):
        for b in range(3):
            taps[a * 3 + b] = taps_ref[a, b, :, own_lanes].astype(jnp.float32)

    for part in range(2):
        for g in (-1, 1):
            pl.when(p_there[-g])(row_copy(g, part).wait_recv)
            for d in (-1, 1):
                first = (lead == 1) if d < 0 else (lead == 0)
                mine = first if part == 0 else jnp.logical_not(first)
                ready = jnp.logical_and(jnp.logical_and(p_there[-g], f_there[d]), mine)
                pl.when(ready)(corner_copy(d, g).start)
    for d in (-1, 1):
        pl.when(f_there[-d])(frame_copy(d).wait_recv)

    col = lax.broadcasted_iota(jnp.int32, (cols, LANES), 0)

    def mix_copy(part, r, t):
        i = order[part] * rows + r
        return pltpu.make_async_remote_copy(
            src_ref=mixed.at[i, t],
            dst_ref=mixed.at[i, t],
            send_sem=mix_send.at[part * rows + r],
            recv_sem=mix_recv.at[part * rows + r],
            device_id=(f_me, p_me, t_peer),
            device_id_type=MESH,
        )

    for part in range(2):
        f = order[part]
        for d in (-1, 1):
            for g in (-1, 1):
                needs = (f == 0) if d > 0 else (f == frames - 1)
                ready = jnp.logical_and(jnp.logical_and(p_there[-g], f_there[-d]), needs)
                pl.when(ready)(corner_copy(d, g).wait_recv)
        for r in range(rows):

            def conv(step, carry):
                at = pl.ds(pl.multiple_of(step * LANES, LANES), LANES)
                sums = [jnp.zeros((cols, LANES), jnp.float32) for _ in range(3)]
                centre = None
                for a in range(3):
                    for b in range(3):
                        x = pad[f + a, r + b, :, at].astype(jnp.float32)
                        if a == 1 and b == 1:
                            centre = x
                        w = taps[a * 3 + b, :, at]
                        for c in range(3):
                            sums[c] = sums[c] + x * w[c : c + 1]
                before = jnp.where(col == 0, 0.0, pltpu.roll(sums[0], 1, 0))
                after = jnp.where(col == cols - 1, 0.0, pltpu.roll(sums[2], cols - 1, 0))
                total = centre + (sums[1] + (before + after))
                mixed[f * rows + r, t_me, :, at] = total.astype(jnp.bfloat16)
                return carry

            lax.fori_loop(0, channels // LANES, conv, 0)
            mix_copy(part, r, t_me).start()

    started = []

    def go(src, dst, s_sem, r_sem, p):
        copy = pltpu.make_async_remote_copy(
            src_ref=src,
            dst_ref=dst,
            send_sem=s_sem,
            recv_sem=r_sem,
            device_id=(f_me, p, t_me),
            device_id_type=MESH,
        )
        copy.start()
        started.append(copy)
        return copy

    pieces = [(0, pl.ds(0, heads))] + [(1, pl.ds(h, 1)) for h in range(heads)]
    arrivals = {}

    def beside(n, slot):
        part, hs = pieces[n]
        at = pl.ds(part * half, half)
        arrivals[n, slot + 1] = go(
            kv_all.at[hs, slot, at],
            kv_all.at[hs, slot + 1, at],
            c_send.at[n, slot // 2],
            c_recv.at[n, slot // 2],
            p_twin,
        )

    def spread_piece(n):
        part, hs = pieces[n]
        at = pl.ds(part * half, half)
        size = heads if part == 0 else 1
        first = 0 if part == 0 else n - 1
        mine = pl.ds(side * heads + first, size)
        other = pl.ds((1 - side) * heads + first, size)
        for m, k in enumerate(far):
            for slot, src in ((0, mine), (2, other)):
                arrivals[n, k + slot] = go(
                    kv_own.at[src, at],
                    kv_all.at[hs, k + slot, at],
                    b_send.at[n, 2 * m + slot // 2],
                    b_recv.at[n, 2 * m + slot // 2],
                    flip(p_me, k + slot),
                )
        arrivals[n, 2] = go(
            kv_own.at[other, at], kv_all.at[hs, 2, at], a_send.at[n], a_recv.at[n], p_pair
        )
        beside(n, 0)

    for part in range(2):
        f = order[part]
        if part == 0:
            loads[3].wait()
            loads[4].wait()
        picked = mod_ref[ts_ref[f]].astype(jnp.float32)
        shift, scale = picked[0:1], 1.0 + picked[1:2]
        for r in range(rows):
            mix_copy(part, r, t_peer).wait_recv()
            xs = [mixed[f * rows + r, t].astype(jnp.float32) for t in range(n_tp)]
            mean = sum(jnp.sum(x, axis=1, keepdims=True) for x in xs) * (1.0 / width)
            xs = [x - mean for x in xs]
            var = sum(jnp.sum(x * x, axis=1, keepdims=True) for x in xs) * (1.0 / width)
            inv = 1.0 / jnp.sqrt(var + 1e-06)
            for t in range(n_tp):
                at = slice(t * channels, (t + 1) * channels)
                y = xs[t] * inv * scale[:, at] + shift[:, at]
                row = part * half + r * cols
                normed[row : row + cols, at] = y.astype(jnp.bfloat16)
        if part == 0:
            loads[5].wait()
            loads[6].wait()
        at = slice(part * half, (part + 1) * half)
        kv = jnp.dot(normed[at], wkv[...], preferred_element_type=jnp.float32)
        for h in range(local_heads):
            k_at = h * HEAD_DIM
            v_at = local_width + h * HEAD_DIM
            kv_own[h, at] = jnp.concatenate(
                [kv[:, k_at : k_at + HEAD_DIM], kv[:, v_at : v_at + HEAD_DIM]], axis=1
            ).astype(jnp.bfloat16)
        for h in range(heads):
            kv_all[h, 0, at] = kv_own[side * heads + h, at]
        for n, (piece_part, _) in enumerate(pieces):
            if piece_part == part:
                spread_piece(n)

    def relay(n):
        for slot in [2] + [k + s for k in far for s in (0, 2)]:
            arrivals[n, slot].wait_recv()
            beside(n, slot)

    relay(0)

    loads[7].wait()
    q = jnp.dot(normed[...], wq[...], preferred_element_type=jnp.float32)
    q = q.astype(jnp.bfloat16).astype(jnp.float32) * (HEAD_DIM**-0.5)
    blank = jnp.zeros((tokens, HEAD_DIM), jnp.float32)
    for h in range(local_heads):
        q_h = q[:, h * HEAD_DIM : (h + 1) * HEAD_DIM]
        q_own[h] = jnp.concatenate([q_h, blank], axis=1).astype(jnp.bfloat16)
        q_pack[h] = jnp.concatenate([q_h[:half], q_h[half:]], axis=1).astype(jnp.bfloat16)
    q_copy = go(
        q_pack.at[pl.ds((1 - side) * heads, heads)], q_peer, q_send.at[0], q_recv.at[0], p_pair
    )

    for n in range(1, len(pieces)):
        relay(n)

    q_copy.wait_recv()
    for slot in range(1, n_patch, 2):
        arrivals[0, slot].wait_recv()
    o_copies = []
    own = []
    zeros = jnp.zeros((half, HEAD_DIM), jnp.float32)
    for h in range(heads):
        for slot in range(1, n_patch, 2):
            arrivals[h + 1, slot].wait_recv()
        packed = q_peer[h].astype(jnp.float32)
        peer = jnp.concatenate(
            [
                jnp.concatenate([packed[:, :HEAD_DIM], zeros], axis=1),
                jnp.concatenate([packed[:, HEAD_DIM:], zeros], axis=1),
            ],
            axis=0,
        ).astype(jnp.bfloat16)
        queries = jnp.concatenate([peer, q_own[side * heads + h]], axis=0)
        rows_kv = kv_all[h].reshape(n_patch * tokens, 2 * HEAD_DIM)
        scores = lax.dot_general(
            queries, rows_kv, (((1,), (1,)), ((), ())), preferred_element_type=jnp.float32
        )
        exps = jnp.exp(scores - jnp.max(scores, axis=1, keepdims=True))
        totals = jnp.sum(exps, axis=1, keepdims=True)
        summed = jnp.dot(
            exps.astype(jnp.bfloat16), rows_kv, preferred_element_type=jnp.float32
        )
        result = summed[:, HEAD_DIM:] / totals
        o_pack[h] = jnp.concatenate(
            [result[:half], result[half:tokens]], axis=1
        ).astype(jnp.bfloat16)
        o_copies.append(go(o_pack.at[h], o_peer.at[h], o_send.at[h], o_recv.at[h], p_pair))
        own.append(result[tokens:])

    for d in (-1, 1):
        for part in range(2):
            pl.when(p_there[d])(row_copy(d, part).wait_send)
        pl.when(f_there[d])(frame_copy(d).wait_send)
        for g in (-1, 1):
            pl.when(jnp.logical_and(p_there[-g], f_there[d]))(corner_copy(d, g).wait_send)
    for part in range(2):
        for r in range(rows):
            mix_copy(part, r, t_me).wait_send()
    for copy in started:
        copy.wait_send()

    others = []
    for h in range(heads):
        o_copies[h].wait_recv()
        packed = o_peer[h].astype(jnp.float32)
        others.append(jnp.concatenate([packed[:, :HEAD_DIM], packed[:, HEAD_DIM:]], axis=0))
    low = jnp.concatenate(own + others, axis=1)
    high = jnp.concatenate(others + own, axis=1)
    final = jnp.where(side == 0, low, high).astype(jnp.bfloat16)
    for part in range(2):
        piece = final[part * half : (part + 1) * half]
        out_ref[order[part]] = piece.reshape(rows, cols, local_width)


def solution(mesh):
    sizes = tuple(mesh.shape[a] for a in ("frame", "patch", "tp"))
    n_patch = sizes[1]
    far = max(1, n_patch // 4 - 1)

    def local(codes, exps, taps, timestep, modulation, wq, wk, wv):
        frames, rows, cols, channels = codes.shape
        tokens = frames * rows * cols
        width, local_width = wq.shape
        local_heads = local_width // HEAD_DIM
        heads = local_heads // 2
        exps = jnp.transpose(exps, (0, 3, 1, 2))
        bf, f32 = jnp.bfloat16, jnp.float32
        hbm = pl.BlockSpec(memory_space=pltpu.HBM)
        dma = pltpu.SemaphoreType.DMA
        macs = tokens * width * local_width * 3
        macs += 2 * tokens * tokens * n_patch * local_heads * 2 * HEAD_DIM
        return pl.pallas_call(
            functools.partial(kernel, sizes),
            out_shape=jax.ShapeDtypeStruct((frames, rows, cols, local_width), bf),
            in_specs=[hbm] * 8,
            out_specs=pl.BlockSpec(memory_space=pltpu.VMEM),
            scratch_shapes=[
                pltpu.SMEM(timestep.shape, jnp.int32),
                pltpu.VMEM(codes.shape, jnp.int32),
                pltpu.VMEM(exps.shape, jnp.int32),
                pltpu.VMEM(taps.shape, bf),
                pltpu.VMEM(modulation.shape, bf),
                pltpu.VMEM((frames + 2, rows + 2, cols, channels), bf),
                pltpu.VMEM((9, 3, channels), f32),
                pltpu.VMEM((frames * rows, sizes[2], cols, channels), bf),
                pltpu.VMEM((tokens, width), bf),
                pltpu.VMEM((width, 2 * local_width), bf),
                pltpu.VMEM((width, local_width), bf),
                pltpu.VMEM((local_heads, tokens, LANES), bf),
                pltpu.VMEM((heads, n_patch, tokens, LANES), bf),
                pltpu.VMEM((local_heads, tokens, LANES), bf),
                pltpu.VMEM((local_heads, tokens // 2, LANES), bf),
                pltpu.VMEM((heads, tokens // 2, LANES), bf),
                pltpu.VMEM((heads, tokens // 2, LANES), bf),
                pltpu.VMEM((heads, tokens // 2, LANES), bf),
                dma((8,)),
                dma((4,)),
                dma((4,)),
                dma((2,)),
                dma((2,)),
                dma((4,)),
                dma((4,)),
                dma((frames * rows,)),
                dma((frames * rows,)),
                dma((heads + 1,)),
                dma((heads + 1,)),
                dma((heads + 1, 2 * far)),
                dma((heads + 1, 2 * far)),
                dma((heads + 1, n_patch // 2)),
                dma((heads + 1, n_patch // 2)),
                dma((1,)),
                dma((1,)),
                dma((heads,)),
                dma((heads,)),
            ],
            compiler_params=pltpu.CompilerParams(
                collective_id=0, has_side_effects=True, vmem_limit_bytes=56 * 1024 * 1024
            ),
            cost_estimate=pl.CostEstimate(
                flops=2 * macs, bytes_accessed=width * local_width * 6, transcendentals=0
            ),
        )(timestep, codes, exps, taps, modulation, wq, wk, wv)

    in_specs = (
        P("frame", "patch", None, "tp"),
        P("frame", "patch", None, "tp"),
        P(),
        P("frame"),
        P(),
        P(None, "tp"),
        P(None, "tp"),
        P(None, "tp"),
    )
    out_specs = P("frame", "patch", None, "tp")
    return jax.shard_map(local, mesh=mesh, in_specs=in_specs, out_specs=out_specs, check_vma=False)
```

```python
import functools

import jax
import jax.numpy as jnp
from jax import lax
from jax.experimental import pallas as pl
from jax.experimental.pallas import tpu as pltpu
from jax.sharding import PartitionSpec as P

HEAD_DIM = 64
LANES = 128
MESH = pl.DeviceIdType.MESH


def flip(index, mask):
    bit = 1
    while bit <= mask:
        if mask & bit:
            index = index + bit - 2 * bit * lax.rem(lax.div(index, bit), 2)
        bit *= 2
    return index


def kernel(
    sizes,
    ts_hbm,
    codes_hbm,
    exps_hbm,
    taps_hbm,
    mod_hbm,
    wq_hbm,
    wk_hbm,
    wv_hbm,
    out_ref,
    ts_ref,
    codes_ref,
    exps_ref,
    taps_ref,
    mod_ref,
    pad,
    taps,
    mixed,
    normed,
    wkv,
    wq,
    kv_own,
    kv_all,
    q_own,
    q_pack,
    q_peer,
    o_pack,
    o_peer,
    in_sem,
    row_send,
    row_recv,
    frame_send,
    frame_recv,
    corner_send,
    corner_recv,
    mix_send,
    mix_recv,
    a_send,
    a_recv,
    b_send,
    b_recv,
    c_send,
    c_recv,
    q_send,
    q_recv,
    o_send,
    o_recv,
):
    n_frame, n_patch, n_tp = sizes
    frames, rows, cols, channels = codes_ref.shape
    tokens = frames * rows * cols
    half = tokens // 2
    local_width = wq_hbm.shape[1]
    local_heads = local_width // HEAD_DIM
    heads = local_heads // 2
    width = n_tp * channels
    f_me = lax.axis_index("frame")
    p_me = lax.axis_index("patch")
    t_me = lax.axis_index("tp")
    t_peer = 1 - t_me
    side = lax.rem(lax.div(p_me, 2), 2)
    p_odd = lax.rem(p_me, 2)
    f_odd = lax.rem(f_me, 2)
    order = (1 - p_odd, p_odd)
    edge = ((rows + 1) * (1 - p_odd), (rows + 1) * p_odd)
    p_next = p_me - 1 + 2 * p_odd
    next_there = jnp.logical_and(p_next >= 0, p_next < n_patch)
    p_pair = flip(p_me, 2)
    p_twin = flip(p_me, 1)
    far = list(range(4, n_patch, 4))

    loads = [
        pltpu.make_async_copy(src, dst, in_sem.at[i])
        for i, (src, dst) in enumerate(
            [
                (codes_hbm.at[:, order[0]], codes_ref.at[:, order[0]]),
                (exps_hbm, exps_ref),
                (taps_hbm, taps_ref),
                (ts_hbm, ts_ref),
                (mod_hbm, mod_ref),
                (wk_hbm, wkv.at[:, pl.ds(0, local_width)]),
                (wv_hbm, wkv.at[:, pl.ds(local_width, local_width)]),
                (wq_hbm, wq),
                (codes_hbm.at[:, order[1]], codes_ref.at[:, order[1]]),
            ]
        )
    ]
    for i in (0, 1, 8, 2, 3, 4, 5, 6, 7):
        loads[i].start()

    barrier = pltpu.get_barrier_semaphore()

    def signal(f, p, t):
        pl.semaphore_signal(barrier, inc=1, device_id=(f, p, t), device_id_type=MESH)

    f_there = {-1: f_me > 0, 1: f_me < n_frame - 1}
    count = 3 + 2 * len(far) + next_there.astype(jnp.int32)
    for d in (-1, 1):

        @pl.when(f_there[d])
        def _():
            signal(f_me + d, p_me, t_me)

        count = count + f_there[d].astype(jnp.int32)

    @pl.when(next_there)
    def _():
        signal(f_me, p_next, t_me)

    signal(f_me, p_me, t_peer)
    signal(f_me, p_pair, t_me)
    signal(f_me, p_twin, t_me)
    for k in far:
        signal(f_me, flip(p_me, k), t_me)
        signal(f_me, flip(p_me, k + 2), t_me)

    for d in (-1, 1):

        @pl.when(jnp.logical_not(f_there[d]))
        def _():
            pad[0 if d < 0 else frames + 1] = jnp.zeros((rows + 2, cols, channels), jnp.bfloat16)

    @pl.when(jnp.logical_not(next_there))
    def _():
        for f in range(frames + 2):
            pad[f, edge[1]] = jnp.zeros((cols, channels), jnp.bfloat16)

    groups = exps_ref.shape[1]
    span = channels // groups
    spread = (
        lax.broadcasted_iota(jnp.int32, (groups, channels), 1) // span
        == lax.broadcasted_iota(jnp.int32, (groups, channels), 0)
    ).astype(jnp.float32).astype(jnp.bfloat16)
    loads[1].wait()

    def dequantize(part):
        r = order[part]
        loads[0 if part == 0 else 8].wait()
        for f in range(frames):
            power = jnp.where(r == 0, exps_ref[f, :, 0, :], exps_ref[f, :, 1, :])
            factor = jnp.left_shift(jnp.ones((groups, cols), jnp.int32), power + 8)
            factor = (factor.astype(jnp.float32) * (2.0**-8)).astype(jnp.bfloat16)
            factor = lax.dot_general(
                factor, spread, (((0,), (0,)), ((), ())), preferred_element_type=jnp.float32
            )
            values = codes_ref[f, r].astype(jnp.float32) * factor
            pad[f + 1, r + 1] = values.astype(jnp.bfloat16)

    def remote(src, dst, s_sem, r_sem, device):
        return pltpu.make_async_remote_copy(
            src_ref=src,
            dst_ref=dst,
            send_sem=s_sem,
            recv_sem=r_sem,
            device_id=device,
            device_id_type=MESH,
        )

    frame_of = (2 - f_odd, 1 + f_odd)

    def row_copy(part, m, arriving):
        row = edge[part] if arriving else order[part] + 1
        return remote(
            pad.at[frame_of[m], row],
            pad.at[frame_of[m], edge[part] if arriving else rows + 1 - edge[part]],
            row_send.at[2 * part + m],
            row_recv.at[2 * part + m],
            (f_me, p_twin if part == 0 else p_next, t_me),
        )

    f_target = (f_me + 1 - 2 * f_odd, f_me - 1 + 2 * f_odd)
    f_ok = tuple(jnp.logical_and(f >= 0, f < n_frame) for f in f_target)
    f_edge = ((frames + 1) * (1 - f_odd), (frames + 1) * f_odd)

    def frame_copy(part, m, row, arriving, sems, number):
        return remote(
            pad.at[f_edge[m] if arriving else frame_of[m], row],
            pad.at[f_edge[m] if arriving else frames + 1 - f_edge[m], row],
            sems[0].at[number],
            sems[1].at[number],
            (f_target[m], p_me, t_me),
        )

    def side_copy(part, m, arriving):
        sems = (frame_send, frame_recv)
        return frame_copy(part, m, order[part] + 1, arriving, sems, 2 * part + m)

    def corner_copy(part, m, arriving):
        sems = (corner_send, corner_recv)
        return frame_copy(part, m, edge[part], arriving, sems, 2 * part + m)

    def when(condition, action):
        if condition is None:
            action()
        else:
            pl.when(condition)(action)

    row_ok = (None, next_there)

    def corner_ok(part, m):
        return f_ok[m] if part == 0 else jnp.logical_and(next_there, f_ok[m])

    def send_rows(part):
        for m in range(2):
            when(row_ok[part], row_copy(part, m, False).start)

    for part in range(2):
        dequantize(part)
        if part == 0:
            pl.semaphore_wait(barrier, count)
            send_rows(0)
        for m in range(2):
            when(f_ok[m], side_copy(part, m, False).start)

    loads[2].wait()
    own_lanes = pl.ds(pl.multiple_of(t_me * channels, LANES), channels)
    for a in range(3):
        for b in range(3):
            taps[a * 3 + b] = taps_ref[a, b, :, own_lanes].astype(jnp.float32)

    for m in range(2):
        row_copy(0, m, False).wait_send()
    send_rows(1)

    col = lax.broadcasted_iota(jnp.int32, (cols, LANES), 0)

    def mix_copy(part, f, t):
        i = f * rows + order[part]
        return pltpu.make_async_remote_copy(
            src_ref=mixed.at[i, t],
            dst_ref=mixed.at[i, t],
            send_sem=mix_send.at[part * frames + f],
            recv_sem=mix_recv.at[part * frames + f],
            device_id=(f_me, p_me, t_peer),
            device_id_type=MESH,
        )

    for part in range(2):
        r = order[part]
        for m in range(2):
            when(row_ok[part], row_copy(part, m, True).wait_recv)
            when(corner_ok(part, m), corner_copy(part, m, False).start)
        if part == 0:
            for both in range(2):
                for m in range(2):
                    when(f_ok[m], side_copy(both, m, True).wait_recv)
        for m in range(2):
            when(corner_ok(part, m), corner_copy(part, m, True).wait_recv)
        for f in range(frames):

            def conv(step, carry):
                at = pl.ds(pl.multiple_of(step * LANES, LANES), LANES)
                sums = [jnp.zeros((cols, LANES), jnp.float32) for _ in range(3)]
                centre = None
                for a in range(3):
                    for b in range(3):
                        x = pad[f + a, r + b, :, at].astype(jnp.float32)
                        if a == 1 and b == 1:
                            centre = x
                        w = taps[a * 3 + b, :, at]
                        for c in range(3):
                            sums[c] = sums[c] + x * w[c : c + 1]
                before = jnp.where(col == 0, 0.0, pltpu.roll(sums[0], 1, 0))
                after = jnp.where(col == cols - 1, 0.0, pltpu.roll(sums[2], cols - 1, 0))
                total = centre + (sums[1] + (before + after))
                mixed[f * rows + r, t_me, :, at] = total.astype(jnp.bfloat16)
                return carry

            lax.fori_loop(0, channels // LANES, conv, 0)
            mix_copy(part, f, t_me).start()

    started = []

    def go(src, dst, s_sem, r_sem, p):
        copy = pltpu.make_async_remote_copy(
            src_ref=src,
            dst_ref=dst,
            send_sem=s_sem,
            recv_sem=r_sem,
            device_id=(f_me, p, t_me),
            device_id_type=MESH,
        )
        copy.start()
        started.append(copy)
        return copy

    pieces = [(0, pl.ds(0, heads))] + [(1, pl.ds(h, 1)) for h in range(heads)]
    arrivals = {}

    def beside(n, slot):
        part, hs = pieces[n]
        at = pl.ds(part * half, half)
        arrivals[n, slot + 1] = go(
            kv_all.at[hs, slot, at],
            kv_all.at[hs, slot + 1, at],
            c_send.at[n, slot // 2],
            c_recv.at[n, slot // 2],
            p_twin,
        )

    def spread_piece(n):
        part, hs = pieces[n]
        at = pl.ds(part * half, half)
        size = heads if part == 0 else 1
        first = 0 if part == 0 else n - 1
        mine = pl.ds(side * heads + first, size)
        other = pl.ds((1 - side) * heads + first, size)
        for m, k in enumerate(far):
            for slot, src in ((0, mine), (2, other)):
                arrivals[n, k + slot] = go(
                    kv_own.at[src, at],
                    kv_all.at[hs, k + slot, at],
                    b_send.at[n, 2 * m + slot // 2],
                    b_recv.at[n, 2 * m + slot // 2],
                    flip(p_me, k + slot),
                )
        arrivals[n, 2] = go(
            kv_own.at[other, at], kv_all.at[hs, 2, at], a_send.at[n], a_recv.at[n], p_pair
        )
        beside(n, 0)

    loads[3].wait()
    loads[4].wait()
    picked = [mod_ref[ts_ref[f]].astype(jnp.float32) for f in range(frames)]
    for part in range(2):
        r = order[part]
        for f in range(frames):
            shift, scale = picked[f][0:1], 1.0 + picked[f][1:2]
            mix_copy(part, f, t_peer).wait_recv()
            xs = [mixed[f * rows + r, t].astype(jnp.float32) for t in range(n_tp)]
            mean = sum(jnp.sum(x, axis=1, keepdims=True) for x in xs) * (1.0 / width)
            xs = [x - mean for x in xs]
            var = sum(jnp.sum(x * x, axis=1, keepdims=True) for x in xs) * (1.0 / width)
            inv = 1.0 / jnp.sqrt(var + 1e-06)
            for t in range(n_tp):
                at = slice(t * channels, (t + 1) * channels)
                y = xs[t] * inv * scale[:, at] + shift[:, at]
                row = part * half + f * cols
                normed[row : row + cols, at] = y.astype(jnp.bfloat16)
        if part == 0:
            loads[5].wait()
            loads[6].wait()
        at = slice(part * half, (part + 1) * half)
        kv = jnp.dot(normed[at], wkv[...], preferred_element_type=jnp.float32)
        for h in range(local_heads):
            k_at = h * HEAD_DIM
            v_at = local_width + h * HEAD_DIM
            kv_own[h, at] = jnp.concatenate(
                [kv[:, k_at : k_at + HEAD_DIM], kv[:, v_at : v_at + HEAD_DIM]], axis=1
            ).astype(jnp.bfloat16)
        for h in range(heads):
            kv_all[h, 0, at] = kv_own[side * heads + h, at]
        for n, (piece_part, _) in enumerate(pieces):
            if piece_part == part:
                spread_piece(n)

    def relay(n, slots):
        for slot in slots:
            arrivals[n, slot].wait_recv()
            beside(n, slot)

    far_slots = [k + s for k in far for s in (0, 2)]
    relay(0, [2])

    loads[7].wait()
    q = jnp.dot(normed[...], wq[...], preferred_element_type=jnp.float32)
    q = q.astype(jnp.bfloat16).astype(jnp.float32) * (HEAD_DIM**-0.5)
    blank = jnp.zeros((tokens, HEAD_DIM), jnp.float32)
    for h in range(local_heads):
        q_h = q[:, h * HEAD_DIM : (h + 1) * HEAD_DIM]
        q_own[h] = jnp.concatenate([q_h, blank], axis=1).astype(jnp.bfloat16)
        q_pack[h] = jnp.concatenate([q_h[:half], q_h[half:]], axis=1).astype(jnp.bfloat16)
    q_copy = go(
        q_pack.at[pl.ds((1 - side) * heads, heads)], q_peer, q_send.at[0], q_recv.at[0], p_pair
    )

    relay(0, far_slots)
    zeros = jnp.zeros((half, HEAD_DIM), jnp.float32)

    def attend(queries, rows_kv, state):
        scores = lax.dot_general(
            queries, rows_kv, (((1,), (1,)), ((), ())), preferred_element_type=jnp.float32
        )
        top = jnp.max(scores, axis=1, keepdims=True)
        if state is not None:
            top = jnp.maximum(top, state[0])
        exps = jnp.exp(scores - top)
        total = jnp.sum(exps, axis=1, keepdims=True)
        summed = jnp.dot(
            exps.astype(jnp.bfloat16), rows_kv, preferred_element_type=jnp.float32
        )
        if state is not None:
            rescale = jnp.exp(state[0] - top)
            total = total + state[1] * rescale
            summed = summed + state[2] * rescale
        return top, total, summed

    def queries_of(h):
        packed = q_peer[h].astype(jnp.float32)
        peer = jnp.concatenate(
            [
                jnp.concatenate([packed[:, :HEAD_DIM], zeros], axis=1),
                jnp.concatenate([packed[:, HEAD_DIM:], zeros], axis=1),
            ],
            axis=0,
        ).astype(jnp.bfloat16)
        return jnp.concatenate([peer, q_own[side * heads + h]], axis=0)

    def keys_of(h, part):
        block = kv_all[h, :, part * half : (part + 1) * half]
        return block.reshape(n_patch * half, 2 * HEAD_DIM)

    queries = []
    states = []
    for h in range(heads):
        relay(h + 1, [2] + far_slots)
        if h == 0:
            q_copy.wait_recv()
            for slot in range(1, n_patch, 2):
                arrivals[0, slot].wait_recv()
        queries.append(queries_of(h))
        states.append(attend(queries[h], keys_of(h, 0), None))

    o_copies = []
    own = []
    for h in range(heads):
        for slot in range(1, n_patch, 2):
            arrivals[h + 1, slot].wait_recv()
        _, total, summed = attend(queries[h], keys_of(h, 1), states[h])
        result = summed[:, HEAD_DIM:] / total
        o_pack[h] = jnp.concatenate(
            [result[:half], result[half:tokens]], axis=1
        ).astype(jnp.bfloat16)
        o_copies.append(go(o_pack.at[h], o_peer.at[h], o_send.at[h], o_recv.at[h], p_pair))
        own.append(result[tokens:])

    for part in range(2):
        for m in range(2):
            if part == 1:
                when(row_ok[part], row_copy(part, m, False).wait_send)
            when(f_ok[m], side_copy(part, m, False).wait_send)
            when(corner_ok(part, m), corner_copy(part, m, False).wait_send)
        for f in range(frames):
            mix_copy(part, f, t_me).wait_send()
    for copy in started:
        copy.wait_send()

    others = []
    for h in range(heads):
        o_copies[h].wait_recv()
        packed = o_peer[h].astype(jnp.float32)
        others.append(jnp.concatenate([packed[:, :HEAD_DIM], packed[:, HEAD_DIM:]], axis=0))
    low = jnp.concatenate(own + others, axis=1)
    high = jnp.concatenate(others + own, axis=1)
    final = jnp.where(side == 0, low, high).astype(jnp.bfloat16)
    for part in range(2):
        for f in range(frames):
            row = part * half + f * cols
            out_ref[f, order[part]] = final[row : row + cols]


def solution(mesh):
    sizes = tuple(mesh.shape[a] for a in ("frame", "patch", "tp"))
    n_patch = sizes[1]
    far = max(1, n_patch // 4 - 1)

    def local(codes, exps, taps, timestep, modulation, wq, wk, wv):
        frames, rows, cols, channels = codes.shape
        tokens = frames * rows * cols
        width, local_width = wq.shape
        local_heads = local_width // HEAD_DIM
        heads = local_heads // 2
        exps = jnp.transpose(exps, (0, 3, 1, 2))
        bf, f32 = jnp.bfloat16, jnp.float32
        hbm = pl.BlockSpec(memory_space=pltpu.HBM)
        dma = pltpu.SemaphoreType.DMA
        macs = tokens * width * local_width * 3
        macs += 2 * tokens * tokens * n_patch * local_heads * 2 * HEAD_DIM
        return pl.pallas_call(
            functools.partial(kernel, sizes),
            out_shape=jax.ShapeDtypeStruct((frames, rows, cols, local_width), bf),
            in_specs=[hbm] * 8,
            out_specs=pl.BlockSpec(memory_space=pltpu.VMEM),
            scratch_shapes=[
                pltpu.SMEM(timestep.shape, jnp.int32),
                pltpu.VMEM(codes.shape, jnp.int32),
                pltpu.VMEM(exps.shape, jnp.int32),
                pltpu.VMEM(taps.shape, bf),
                pltpu.VMEM(modulation.shape, bf),
                pltpu.VMEM((frames + 2, rows + 2, cols, channels), bf),
                pltpu.VMEM((9, 3, channels), f32),
                pltpu.VMEM((frames * rows, sizes[2], cols, channels), bf),
                pltpu.VMEM((tokens, width), bf),
                pltpu.VMEM((width, 2 * local_width), bf),
                pltpu.VMEM((width, local_width), bf),
                pltpu.VMEM((local_heads, tokens, LANES), bf),
                pltpu.VMEM((heads, n_patch, tokens, LANES), bf),
                pltpu.VMEM((local_heads, tokens, LANES), bf),
                pltpu.VMEM((local_heads, tokens // 2, LANES), bf),
                pltpu.VMEM((heads, tokens // 2, LANES), bf),
                pltpu.VMEM((heads, tokens // 2, LANES), bf),
                pltpu.VMEM((heads, tokens // 2, LANES), bf),
                dma((9,)),
                dma((4,)),
                dma((4,)),
                dma((4,)),
                dma((4,)),
                dma((4,)),
                dma((4,)),
                dma((frames * rows,)),
                dma((frames * rows,)),
                dma((heads + 1,)),
                dma((heads + 1,)),
                dma((heads + 1, 2 * far)),
                dma((heads + 1, 2 * far)),
                dma((heads + 1, n_patch // 2)),
                dma((heads + 1, n_patch // 2)),
                dma((1,)),
                dma((1,)),
                dma((heads,)),
                dma((heads,)),
            ],
            compiler_params=pltpu.CompilerParams(
                collective_id=0, has_side_effects=True, vmem_limit_bytes=56 * 1024 * 1024
            ),
            cost_estimate=pl.CostEstimate(
                flops=2 * macs, bytes_accessed=width * local_width * 6, transcendentals=0
            ),
        )(timestep, codes, exps, taps, modulation, wq, wk, wv)

    in_specs = (
        P("frame", "patch", None, "tp"),
        P("frame", "patch", None, "tp"),
        P(),
        P("frame"),
        P(),
        P(None, "tp"),
        P(None, "tp"),
        P(None, "tp"),
    )
    out_specs = P("frame", "patch", None, "tp")
    return jax.shard_map(local, mesh=mesh, in_specs=in_specs, out_specs=out_specs, check_vma=False)
```

```python
import functools

import jax
import jax.numpy as jnp
from jax import lax
from jax.experimental import pallas as pl
from jax.experimental.pallas import tpu as pltpu
from jax.sharding import PartitionSpec as P

HEAD_DIM = 64
LANES = 128
MESH = pl.DeviceIdType.MESH


def flip(index, mask):
    bit = 1
    while bit <= mask:
        if mask & bit:
            index = index + bit - 2 * bit * lax.rem(lax.div(index, bit), 2)
        bit *= 2
    return index


def kernel(
    sizes,
    ts_hbm,
    codes_hbm,
    exps_hbm,
    taps_hbm,
    mod_hbm,
    wq_hbm,
    wk_hbm,
    wv_hbm,
    out_ref,
    ts_ref,
    codes_ref,
    exps_ref,
    taps_ref,
    mod_ref,
    pad,
    taps,
    mixed,
    normed,
    wkv,
    wq,
    kv_own,
    kv_all,
    q_own,
    q_pack,
    q_peer,
    o_pack,
    o_peer,
    in_sem,
    row_send,
    row_recv,
    frame_send,
    frame_recv,
    corner_send,
    corner_recv,
    mix_send,
    mix_recv,
    a_send,
    a_recv,
    b_send,
    b_recv,
    c_send,
    c_recv,
    q_send,
    q_recv,
    o_send,
    o_recv,
):
    n_frame, n_patch, n_tp = sizes
    frames, rows, cols, channels = codes_ref.shape
    tokens = frames * rows * cols
    half = rows * cols
    local_width = wq_hbm.shape[1]
    local_heads = local_width // HEAD_DIM
    heads = local_heads // 2
    width = n_tp * channels
    f_me = lax.axis_index("frame")
    p_me = lax.axis_index("patch")
    t_me = lax.axis_index("tp")
    t_peer = 1 - t_me
    side = lax.rem(lax.div(p_me, 2), 2)
    lead = lax.rem(f_me, 2)
    order = (lead, 1 - lead)
    p_pair = flip(p_me, 2)
    p_twin = flip(p_me, 1)
    p_cross = flip(p_me, 3)
    far = list(range(4, n_patch, 4))

    loads = [
        pltpu.make_async_copy(src, dst, in_sem.at[i])
        for i, (src, dst) in enumerate(
            [
                (codes_hbm, codes_ref),
                (exps_hbm, exps_ref),
                (taps_hbm, taps_ref),
                (ts_hbm, ts_ref),
                (mod_hbm, mod_ref),
                (wk_hbm, wkv.at[:, pl.ds(0, local_width)]),
                (wv_hbm, wkv.at[:, pl.ds(local_width, local_width)]),
                (wq_hbm, wq),
            ]
        )
    ]
    for copy in loads[:2]:
        copy.start()

    barrier = pltpu.get_barrier_semaphore()

    def signal(f, p, t):
        pl.semaphore_signal(barrier, inc=1, device_id=(f, p, t), device_id_type=MESH)

    f_there = {-1: f_me > 0, 1: f_me < n_frame - 1}
    p_there = {-1: p_me > 0, 1: p_me < n_patch - 1}
    count = 4 + 2 * len(far)
    for d in (-1, 1):

        @pl.when(f_there[d])
        def _():
            signal(f_me + d, p_me, t_me)

        @pl.when(p_there[d])
        def _():
            signal(f_me, p_me + d, t_me)

        count = count + f_there[d].astype(jnp.int32) + p_there[d].astype(jnp.int32)
    signal(f_me, p_me, t_peer)
    signal(f_me, p_pair, t_me)
    signal(f_me, p_twin, t_me)
    signal(f_me, p_cross, t_me)
    for k in far:
        signal(f_me, flip(p_me, k), t_me)
        signal(f_me, flip(p_me, k + 2), t_me)
    for copy in loads[2:]:
        copy.start()

    for d in (-1, 1):
        edge_f = 0 if d < 0 else frames + 1
        edge_r = 0 if d < 0 else rows + 1

        @pl.when(jnp.logical_not(f_there[d]))
        def _():
            pad[edge_f] = jnp.zeros((rows + 2, cols, channels), jnp.bfloat16)

        @pl.when(jnp.logical_not(p_there[d]))
        def _():
            pad[1 : 1 + frames, edge_r] = jnp.zeros((frames, cols, channels), jnp.bfloat16)
            for g in (-1, 1):

                @pl.when(f_there[g])
                def _():
                    pad[0 if g < 0 else frames + 1, edge_r] = jnp.zeros(
                        (cols, channels), jnp.bfloat16
                    )

    groups = exps_ref.shape[1]
    span = channels // groups
    spread = (
        lax.broadcasted_iota(jnp.int32, (groups, channels), 1) // span
        == lax.broadcasted_iota(jnp.int32, (groups, channels), 0)
    ).astype(jnp.float32).astype(jnp.bfloat16)
    loads[0].wait()
    loads[1].wait()
    for f in range(frames):
        for r in range(rows):
            factor = jnp.left_shift(jnp.ones((groups, cols), jnp.int32), exps_ref[f, :, r, :] + 8)
            factor = (factor.astype(jnp.float32) * (2.0**-8)).astype(jnp.bfloat16)
            factor = lax.dot_general(
                factor, spread, (((0,), (0,)), ((), ())), preferred_element_type=jnp.float32
            )
            values = codes_ref[f, r].astype(jnp.float32) * factor
            pad[f + 1, r + 1] = values.astype(jnp.bfloat16)

    pl.semaphore_wait(barrier, count)

    def row_copy(d, part):
        frame = 1 + order[1 - part]
        number = (0 if d < 0 else 2) + part
        return pltpu.make_async_remote_copy(
            src_ref=pad.at[frame, rows if d > 0 else 1],
            dst_ref=pad.at[frame, 0 if d > 0 else rows + 1],
            send_sem=row_send.at[number],
            recv_sem=row_recv.at[number],
            device_id=(f_me, p_me + d, t_me),
            device_id_type=MESH,
        )

    def frame_copy(d):
        number = 0 if d < 0 else 1
        return pltpu.make_async_remote_copy(
            src_ref=pad.at[frames if d > 0 else 1, pl.ds(1, rows)],
            dst_ref=pad.at[0 if d > 0 else frames + 1, pl.ds(1, rows)],
            send_sem=frame_send.at[number],
            recv_sem=frame_recv.at[number],
            device_id=(f_me + d, p_me, t_me),
            device_id_type=MESH,
        )

    def corner_copy(d, g):
        number = (0 if d < 0 else 2) + (0 if g < 0 else 1)
        row = 0 if g > 0 else rows + 1
        return pltpu.make_async_remote_copy(
            src_ref=pad.at[frames if d > 0 else 1, row],
            dst_ref=pad.at[0 if d > 0 else frames + 1, row],
            send_sem=corner_send.at[number],
            recv_sem=corner_recv.at[number],
            device_id=(f_me + d, p_me, t_me),
            device_id_type=MESH,
        )

    for part in range(2):
        for d in (-1, 1):
            pl.when(p_there[d])(row_copy(d, part).start)
    for d in (-1, 1):
        pl.when(f_there[d])(frame_copy(d).start)

    loads[2].wait()
    own_lanes = pl.ds(pl.multiple_of(t_me * channels, LANES), channels)
    for a in range(3):
        for b in range(3):
            taps[a * 3 + b] = taps_ref[a, b, :, own_lanes].astype(jnp.float32)

    for part in range(2):
        for g in (-1, 1):
            pl.when(p_there[-g])(row_copy(g, part).wait_recv)
            for d in (-1, 1):
                first = (lead == 1) if d < 0 else (lead == 0)
                mine = first if part == 0 else jnp.logical_not(first)
                ready = jnp.logical_and(jnp.logical_and(p_there[-g], f_there[d]), mine)
                pl.when(ready)(corner_copy(d, g).start)
    for d in (-1, 1):
        pl.when(f_there[-d])(frame_copy(d).wait_recv)

    col = lax.broadcasted_iota(jnp.int32, (cols, LANES), 0)

    def mix_copy(part, r, t):
        i = order[part] * rows + r
        return pltpu.make_async_remote_copy(
            src_ref=mixed.at[i, t],
            dst_ref=mixed.at[i, t],
            send_sem=mix_send.at[part * rows + r],
            recv_sem=mix_recv.at[part * rows + r],
            device_id=(f_me, p_me, t_peer),
            device_id_type=MESH,
        )

    for part in range(2):
        f = order[part]
        for d in (-1, 1):
            for g in (-1, 1):
                needs = (f == 0) if d > 0 else (f == frames - 1)
                ready = jnp.logical_and(jnp.logical_and(p_there[-g], f_there[-d]), needs)
                pl.when(ready)(corner_copy(d, g).wait_recv)
        for r in range(rows):

            def conv(step, carry):
                at = pl.ds(pl.multiple_of(step * LANES, LANES), LANES)
                sums = [jnp.zeros((cols, LANES), jnp.float32) for _ in range(3)]
                centre = None
                for a in range(3):
                    for b in range(3):
                        x = pad[f + a, r + b, :, at].astype(jnp.float32)
                        if a == 1 and b == 1:
                            centre = x
                        w = taps[a * 3 + b, :, at]
                        for c in range(3):
                            sums[c] = sums[c] + x * w[c : c + 1]
                before = jnp.where(col == 0, 0.0, pltpu.roll(sums[0], 1, 0))
                after = jnp.where(col == cols - 1, 0.0, pltpu.roll(sums[2], cols - 1, 0))
                total = centre + (sums[1] + (before + after))
                mixed[f * rows + r, t_me, :, at] = total.astype(jnp.bfloat16)
                return carry

            lax.fori_loop(0, channels // LANES, conv, 0)
            mix_copy(part, r, t_me).start()

    started = []

    def go(src, dst, s_sem, r_sem, p):
        copy = pltpu.make_async_remote_copy(
            src_ref=src,
            dst_ref=dst,
            send_sem=s_sem,
            recv_sem=r_sem,
            device_id=(f_me, p, t_me),
            device_id_type=MESH,
        )
        copy.start()
        started.append(copy)
        return copy

    pieces = [(0, pl.ds(0, heads))] + [(1, pl.ds(h, 1)) for h in range(heads)]
    arrivals = {}

    def beside(n, slot):
        part, hs = pieces[n]
        at = pl.ds(part * half, half)
        arrivals[n, slot + 1] = go(
            kv_all.at[hs, slot, at],
            kv_all.at[hs, slot + 1, at],
            c_send.at[n, slot // 2],
            c_recv.at[n, slot // 2],
            p_twin,
        )

    def spread_piece(n):
        part, hs = pieces[n]
        at = pl.ds(part * half, half)
        size = heads if part == 0 else 1
        first = 0 if part == 0 else n - 1
        mine = pl.ds(side * heads + first, size)
        other = pl.ds((1 - side) * heads + first, size)
        for m, k in enumerate(far):
            for slot, src in ((0, mine), (2, other)):
                arrivals[n, k + slot] = go(
                    kv_own.at[src, at],
                    kv_all.at[hs, k + slot, at],
                    b_send.at[n, 2 * m + slot // 2],
                    b_recv.at[n, 2 * m + slot // 2],
                    flip(p_me, k + slot),
                )
        arrivals[n, 2] = go(
            kv_own.at[other, at], kv_all.at[hs, 2, at], a_send.at[n], a_recv.at[n], p_pair
        )
        arrivals[n, 3] = go(
            kv_own.at[other, at],
            kv_all.at[hs, 3, at],
            c_send.at[n, 1],
            c_recv.at[n, 1],
            p_cross,
        )
        beside(n, 0)

    for part in range(2):
        f = order[part]
        if part == 0:
            loads[3].wait()
            loads[4].wait()
        picked = mod_ref[ts_ref[f]].astype(jnp.float32)
        shift, scale = picked[0:1], 1.0 + picked[1:2]
        for r in range(rows):
            mix_copy(part, r, t_peer).wait_recv()
            xs = [mixed[f * rows + r, t].astype(jnp.float32) for t in range(n_tp)]
            mean = sum(jnp.sum(x, axis=1, keepdims=True) for x in xs) * (1.0 / width)
            xs = [x - mean for x in xs]
            var = sum(jnp.sum(x * x, axis=1, keepdims=True) for x in xs) * (1.0 / width)
            inv = 1.0 / jnp.sqrt(var + 1e-06)
            for t in range(n_tp):
                at = slice(t * channels, (t + 1) * channels)
                y = xs[t] * inv * scale[:, at] + shift[:, at]
                row = part * half + r * cols
                normed[row : row + cols, at] = y.astype(jnp.bfloat16)
        if part == 0:
            loads[5].wait()
            loads[6].wait()
        at = slice(part * half, (part + 1) * half)
        kv = jnp.dot(normed[at], wkv[...], preferred_element_type=jnp.float32)
        for h in range(local_heads):
            k_at = h * HEAD_DIM
            v_at = local_width + h * HEAD_DIM
            kv_own[h, at] = jnp.concatenate(
                [kv[:, k_at : k_at + HEAD_DIM], kv[:, v_at : v_at + HEAD_DIM]], axis=1
            ).astype(jnp.bfloat16)
        for h in range(heads):
            kv_all[h, 0, at] = kv_own[side * heads + h, at]
        for n, (piece_part, _) in enumerate(pieces):
            if piece_part == part:
                spread_piece(n)

    def relay(n):
        for slot in [k + s for k in far for s in (0, 2)]:
            arrivals[n, slot].wait_recv()
            beside(n, slot)

    loads[7].wait()
    q = jnp.dot(normed[...], wq[...], preferred_element_type=jnp.float32)
    q = q.astype(jnp.bfloat16).astype(jnp.float32) * (HEAD_DIM**-0.5)
    blank = jnp.zeros((tokens, HEAD_DIM), jnp.float32)
    for h in range(local_heads):
        q_h = q[:, h * HEAD_DIM : (h + 1) * HEAD_DIM]
        q_own[h] = jnp.concatenate([q_h, blank], axis=1).astype(jnp.bfloat16)
        q_pack[h] = jnp.concatenate([q_h[:half], q_h[half:]], axis=1).astype(jnp.bfloat16)
    q_copy = go(
        q_pack.at[pl.ds((1 - side) * heads, heads)], q_peer, q_send.at[0], q_recv.at[0], p_pair
    )

    for n in range(len(pieces)):
        relay(n)

    q_copy.wait_recv()
    for slot in [2] + list(range(1, n_patch, 2)):
        arrivals[0, slot].wait_recv()
    o_copies = []
    own = []
    zeros = jnp.zeros((half, HEAD_DIM), jnp.float32)
    for h in range(heads):
        for slot in [2] + list(range(1, n_patch, 2)):
            arrivals[h + 1, slot].wait_recv()
        packed = q_peer[h].astype(jnp.float32)
        peer = jnp.concatenate(
            [
                jnp.concatenate([packed[:, :HEAD_DIM], zeros], axis=1),
                jnp.concatenate([packed[:, HEAD_DIM:], zeros], axis=1),
            ],
            axis=0,
        ).astype(jnp.bfloat16)
        queries = jnp.concatenate([peer, q_own[side * heads + h]], axis=0)
        rows_kv = kv_all[h].reshape(n_patch * tokens, 2 * HEAD_DIM)
        scores = lax.dot_general(
            queries, rows_kv, (((1,), (1,)), ((), ())), preferred_element_type=jnp.float32
        )
        exps = jnp.exp(scores - jnp.max(scores, axis=1, keepdims=True))
        totals = jnp.sum(exps, axis=1, keepdims=True)
        summed = jnp.dot(
            exps.astype(jnp.bfloat16), rows_kv, preferred_element_type=jnp.float32
        )
        result = summed[:, HEAD_DIM:] / totals
        o_pack[h] = jnp.concatenate(
            [result[:half], result[half:tokens]], axis=1
        ).astype(jnp.bfloat16)
        o_copies.append(go(o_pack.at[h], o_peer.at[h], o_send.at[h], o_recv.at[h], p_pair))
        own.append(result[tokens:])

    for d in (-1, 1):
        for part in range(2):
            pl.when(p_there[d])(row_copy(d, part).wait_send)
        pl.when(f_there[d])(frame_copy(d).wait_send)
        for g in (-1, 1):
            pl.when(jnp.logical_and(p_there[-g], f_there[d]))(corner_copy(d, g).wait_send)
    for part in range(2):
        for r in range(rows):
            mix_copy(part, r, t_me).wait_send()
    for copy in started:
        copy.wait_send()

    others = []
    for h in range(heads):
        o_copies[h].wait_recv()
        packed = o_peer[h].astype(jnp.float32)
        others.append(jnp.concatenate([packed[:, :HEAD_DIM], packed[:, HEAD_DIM:]], axis=0))
    low = jnp.concatenate(own + others, axis=1)
    high = jnp.concatenate(others + own, axis=1)
    final = jnp.where(side == 0, low, high).astype(jnp.bfloat16)
    for part in range(2):
        piece = final[part * half : (part + 1) * half]
        out_ref[order[part]] = piece.reshape(rows, cols, local_width)


def solution(mesh):
    sizes = tuple(mesh.shape[a] for a in ("frame", "patch", "tp"))
    n_patch = sizes[1]
    far = max(1, n_patch // 4 - 1)

    def local(codes, exps, taps, timestep, modulation, wq, wk, wv):
        frames, rows, cols, channels = codes.shape
        tokens = frames * rows * cols
        width, local_width = wq.shape
        local_heads = local_width // HEAD_DIM
        heads = local_heads // 2
        exps = jnp.transpose(exps, (0, 3, 1, 2))
        bf, f32 = jnp.bfloat16, jnp.float32
        hbm = pl.BlockSpec(memory_space=pltpu.HBM)
        dma = pltpu.SemaphoreType.DMA
        macs = tokens * width * local_width * 3
        macs += 2 * tokens * tokens * n_patch * local_heads * 2 * HEAD_DIM
        return pl.pallas_call(
            functools.partial(kernel, sizes),
            out_shape=jax.ShapeDtypeStruct((frames, rows, cols, local_width), bf),
            in_specs=[hbm] * 8,
            out_specs=pl.BlockSpec(memory_space=pltpu.VMEM),
            scratch_shapes=[
                pltpu.SMEM(timestep.shape, jnp.int32),
                pltpu.VMEM(codes.shape, jnp.int32),
                pltpu.VMEM(exps.shape, jnp.int32),
                pltpu.VMEM(taps.shape, bf),
                pltpu.VMEM(modulation.shape, bf),
                pltpu.VMEM((frames + 2, rows + 2, cols, channels), bf),
                pltpu.VMEM((9, 3, channels), f32),
                pltpu.VMEM((frames * rows, sizes[2], cols, channels), bf),
                pltpu.VMEM((tokens, width), bf),
                pltpu.VMEM((width, 2 * local_width), bf),
                pltpu.VMEM((width, local_width), bf),
                pltpu.VMEM((local_heads, tokens, LANES), bf),
                pltpu.VMEM((heads, n_patch, tokens, LANES), bf),
                pltpu.VMEM((local_heads, tokens, LANES), bf),
                pltpu.VMEM((local_heads, tokens // 2, LANES), bf),
                pltpu.VMEM((heads, tokens // 2, LANES), bf),
                pltpu.VMEM((heads, tokens // 2, LANES), bf),
                pltpu.VMEM((heads, tokens // 2, LANES), bf),
                dma((8,)),
                dma((4,)),
                dma((4,)),
                dma((2,)),
                dma((2,)),
                dma((4,)),
                dma((4,)),
                dma((frames * rows,)),
                dma((frames * rows,)),
                dma((heads + 1,)),
                dma((heads + 1,)),
                dma((heads + 1, 2 * far)),
                dma((heads + 1, 2 * far)),
                dma((heads + 1, n_patch // 2)),
                dma((heads + 1, n_patch // 2)),
                dma((1,)),
                dma((1,)),
                dma((heads,)),
                dma((heads,)),
            ],
            compiler_params=pltpu.CompilerParams(
                collective_id=0, has_side_effects=True, vmem_limit_bytes=56 * 1024 * 1024
            ),
            cost_estimate=pl.CostEstimate(
                flops=2 * macs, bytes_accessed=width * local_width * 6, transcendentals=0
            ),
        )(timestep, codes, exps, taps, modulation, wq, wk, wv)

    in_specs = (
        P("frame", "patch", None, "tp"),
        P("frame", "patch", None, "tp"),
        P(),
        P("frame"),
        P(),
        P(None, "tp"),
        P(None, "tp"),
        P(None, "tp"),
    )
    out_specs = P("frame", "patch", None, "tp")
    return jax.shard_map(local, mesh=mesh, in_specs=in_specs, out_specs=out_specs, check_vma=False)
```

```python
import functools

import jax
import jax.numpy as jnp
from jax import lax
from jax.experimental import pallas as pl
from jax.experimental.pallas import tpu as pltpu
from jax.sharding import PartitionSpec as P

HEAD_DIM = 64
LANES = 128
MESH = pl.DeviceIdType.MESH


def flip(index, mask):
    bit = 1
    while bit <= mask:
        if mask & bit:
            index = index + bit - 2 * bit * lax.rem(lax.div(index, bit), 2)
        bit *= 2
    return index


def kernel(
    sizes,
    ts_hbm,
    codes_hbm,
    exps_hbm,
    taps_hbm,
    mod_hbm,
    wq_hbm,
    wk_hbm,
    wv_hbm,
    out_ref,
    ts_ref,
    codes_ref,
    exps_ref,
    taps_ref,
    mod_ref,
    pad,
    taps,
    mixed,
    normed,
    wkv,
    wq,
    kv_own,
    kv_all,
    q_own,
    q_pack,
    q_peer,
    o_pack,
    o_peer,
    in_sem,
    row_send,
    row_recv,
    frame_send,
    frame_recv,
    corner_send,
    corner_recv,
    mix_send,
    mix_recv,
    a_send,
    a_recv,
    b_send,
    b_recv,
    c_send,
    c_recv,
    q_send,
    q_recv,
    o_send,
    o_recv,
):
    n_frame, n_patch, n_tp = sizes
    frames, rows, cols, channels = codes_ref.shape
    tokens = frames * rows * cols
    half = rows * cols
    local_width = wq_hbm.shape[1]
    local_heads = local_width // HEAD_DIM
    heads = local_heads // 2
    width = n_tp * channels
    f_me = lax.axis_index("frame")
    p_me = lax.axis_index("patch")
    t_me = lax.axis_index("tp")
    t_peer = 1 - t_me
    side = lax.rem(lax.div(p_me, 2), 2)
    lead = lax.rem(f_me, 2)
    order = (lead, 1 - lead)
    p_pair = flip(p_me, 2)
    p_twin = flip(p_me, 1)
    p_cross = flip(p_me, 3)
    far = list(range(4, n_patch, 4))

    loads = [
        pltpu.make_async_copy(src, dst, in_sem.at[i])
        for i, (src, dst) in enumerate(
            [
                (codes_hbm.at[order[1]], codes_ref.at[order[1]]),
                (exps_hbm, exps_ref),
                (taps_hbm, taps_ref),
                (ts_hbm, ts_ref),
                (mod_hbm, mod_ref),
                (wk_hbm, wkv.at[:, pl.ds(0, local_width)]),
                (wv_hbm, wkv.at[:, pl.ds(local_width, local_width)]),
                (wq_hbm, wq),
                (codes_hbm.at[order[0]], codes_ref.at[order[0]]),
            ]
        )
    ]
    for i in (0, 1, 8):
        loads[i].start()

    barrier = pltpu.get_barrier_semaphore()

    def signal(f, p, t):
        pl.semaphore_signal(barrier, inc=1, device_id=(f, p, t), device_id_type=MESH)

    f_there = {-1: f_me > 0, 1: f_me < n_frame - 1}
    p_there = {-1: p_me > 0, 1: p_me < n_patch - 1}
    count = 4 + 2 * len(far)
    for d in (-1, 1):

        @pl.when(f_there[d])
        def _():
            signal(f_me + d, p_me, t_me)

        @pl.when(p_there[d])
        def _():
            signal(f_me, p_me + d, t_me)

        count = count + f_there[d].astype(jnp.int32) + p_there[d].astype(jnp.int32)
    signal(f_me, p_me, t_peer)
    signal(f_me, p_pair, t_me)
    signal(f_me, p_twin, t_me)
    signal(f_me, p_cross, t_me)
    for k in far:
        signal(f_me, flip(p_me, k), t_me)
        signal(f_me, flip(p_me, k + 2), t_me)
    for copy in loads[2:8]:
        copy.start()

    for d in (-1, 1):
        edge_f = 0 if d < 0 else frames + 1
        edge_r = 0 if d < 0 else rows + 1

        @pl.when(jnp.logical_not(f_there[d]))
        def _():
            pad[edge_f] = jnp.zeros((rows + 2, cols, channels), jnp.bfloat16)

        @pl.when(jnp.logical_not(p_there[d]))
        def _():
            pad[1 : 1 + frames, edge_r] = jnp.zeros((frames, cols, channels), jnp.bfloat16)
            for g in (-1, 1):

                @pl.when(f_there[g])
                def _():
                    pad[0 if g < 0 else frames + 1, edge_r] = jnp.zeros(
                        (cols, channels), jnp.bfloat16
                    )

    groups = exps_ref.shape[1]
    span = channels // groups
    spread = (
        lax.broadcasted_iota(jnp.int32, (groups, channels), 1) // span
        == lax.broadcasted_iota(jnp.int32, (groups, channels), 0)
    ).astype(jnp.float32).astype(jnp.bfloat16)
    loads[1].wait()

    def dequantize(f):
        for r in range(rows):
            factor = jnp.left_shift(jnp.ones((groups, cols), jnp.int32), exps_ref[f, :, r, :] + 8)
            factor = (factor.astype(jnp.float32) * (2.0**-8)).astype(jnp.bfloat16)
            factor = lax.dot_general(
                factor, spread, (((0,), (0,)), ((), ())), preferred_element_type=jnp.float32
            )
            values = codes_ref[f, r].astype(jnp.float32) * factor
            pad[f + 1, r + 1] = values.astype(jnp.bfloat16)

    def row_copy(d, part):
        frame = 1 + order[1 - part]
        number = (0 if d < 0 else 2) + part
        return pltpu.make_async_remote_copy(
            src_ref=pad.at[frame, rows if d > 0 else 1],
            dst_ref=pad.at[frame, 0 if d > 0 else rows + 1],
            send_sem=row_send.at[number],
            recv_sem=row_recv.at[number],
            device_id=(f_me, p_me + d, t_me),
            device_id_type=MESH,
        )

    def frame_copy(d):
        number = 0 if d < 0 else 1
        return pltpu.make_async_remote_copy(
            src_ref=pad.at[frames if d > 0 else 1, pl.ds(1, rows)],
            dst_ref=pad.at[0 if d > 0 else frames + 1, pl.ds(1, rows)],
            send_sem=frame_send.at[number],
            recv_sem=frame_recv.at[number],
            device_id=(f_me + d, p_me, t_me),
            device_id_type=MESH,
        )

    def corner_copy(d, g):
        number = (0 if d < 0 else 2) + (0 if g < 0 else 1)
        row = 0 if g > 0 else rows + 1
        return pltpu.make_async_remote_copy(
            src_ref=pad.at[frames if d > 0 else 1, row],
            dst_ref=pad.at[0 if d > 0 else frames + 1, row],
            send_sem=corner_send.at[number],
            recv_sem=corner_recv.at[number],
            device_id=(f_me + d, p_me, t_me),
            device_id_type=MESH,
        )

    for part in range(2):
        loads[0 if part == 0 else 8].wait()
        dequantize(order[1 - part])
        if part == 0:
            pl.semaphore_wait(barrier, count)
        for d in (-1, 1):
            pl.when(p_there[d])(row_copy(d, part).start)
    for d in (-1, 1):
        pl.when(f_there[d])(frame_copy(d).start)

    loads[2].wait()
    own_lanes = pl.ds(pl.multiple_of(t_me * channels, LANES), channels)
    for a in range(3):
        for b in range(3):
            taps[a * 3 + b] = taps_ref[a, b, :, own_lanes].astype(jnp.float32)

    for part in range(2):
        for g in (-1, 1):
            pl.when(p_there[-g])(row_copy(g, part).wait_recv)
            for d in (-1, 1):
                first = (lead == 1) if d < 0 else (lead == 0)
                mine = first if part == 0 else jnp.logical_not(first)
                ready = jnp.logical_and(jnp.logical_and(p_there[-g], f_there[d]), mine)
                pl.when(ready)(corner_copy(d, g).start)
    for d in (-1, 1):
        pl.when(f_there[-d])(frame_copy(d).wait_recv)

    col = lax.broadcasted_iota(jnp.int32, (cols, LANES), 0)

    def mix_copy(part, r, t):
        i = order[part] * rows + r
        return pltpu.make_async_remote_copy(
            src_ref=mixed.at[i, t],
            dst_ref=mixed.at[i, t],
            send_sem=mix_send.at[part * rows + r],
            recv_sem=mix_recv.at[part * rows + r],
            device_id=(f_me, p_me, t_peer),
            device_id_type=MESH,
        )

    for part in range(2):
        f = order[part]
        for d in (-1, 1):
            for g in (-1, 1):
                needs = (f == 0) if d > 0 else (f == frames - 1)
                ready = jnp.logical_and(jnp.logical_and(p_there[-g], f_there[-d]), needs)
                pl.when(ready)(corner_copy(d, g).wait_recv)
        for r in range(rows):

            def conv(step, carry):
                at = pl.ds(pl.multiple_of(step * LANES, LANES), LANES)
                sums = [jnp.zeros((cols, LANES), jnp.float32) for _ in range(3)]
                centre = None
                for a in range(3):
                    for b in range(3):
                        x = pad[f + a, r + b, :, at].astype(jnp.float32)
                        if a == 1 and b == 1:
                            centre = x
                        w = taps[a * 3 + b, :, at]
                        for c in range(3):
                            sums[c] = sums[c] + x * w[c : c + 1]
                before = jnp.where(col == 0, 0.0, pltpu.roll(sums[0], 1, 0))
                after = jnp.where(col == cols - 1, 0.0, pltpu.roll(sums[2], cols - 1, 0))
                total = centre + (sums[1] + (before + after))
                mixed[f * rows + r, t_me, :, at] = total.astype(jnp.bfloat16)
                return carry

            lax.fori_loop(0, channels // LANES, conv, 0)
            mix_copy(part, r, t_me).start()

    started = []

    def go(src, dst, s_sem, r_sem, p):
        copy = pltpu.make_async_remote_copy(
            src_ref=src,
            dst_ref=dst,
            send_sem=s_sem,
            recv_sem=r_sem,
            device_id=(f_me, p, t_me),
            device_id_type=MESH,
        )
        copy.start()
        started.append(copy)
        return copy

    pieces = [(0, pl.ds(0, heads))] + [(1, pl.ds(h, 1)) for h in range(heads)]
    arrivals = {}

    def beside(n, slot):
        part, hs = pieces[n]
        at = pl.ds(part * half, half)
        arrivals[n, slot + 1] = go(
            kv_all.at[hs, slot, at],
            kv_all.at[hs, slot + 1, at],
            c_send.at[n, slot // 2],
            c_recv.at[n, slot // 2],
            p_twin,
        )

    def spread_piece(n):
        part, hs = pieces[n]
        at = pl.ds(part * half, half)
        size = heads if part == 0 else 1
        first = 0 if part == 0 else n - 1
        mine = pl.ds(side * heads + first, size)
        other = pl.ds((1 - side) * heads + first, size)
        for m, k in enumerate(far):
            for slot, src in ((0, mine), (2, other)):
                arrivals[n, k + slot] = go(
                    kv_own.at[src, at],
                    kv_all.at[hs, k + slot, at],
                    b_send.at[n, 2 * m + slot // 2],
                    b_recv.at[n, 2 * m + slot // 2],
                    flip(p_me, k + slot),
                )
        arrivals[n, 2] = go(
            kv_own.at[other, at], kv_all.at[hs, 2, at], a_send.at[n], a_recv.at[n], p_pair
        )
        arrivals[n, 3] = go(
            kv_own.at[other, at],
            kv_all.at[hs, 3, at],
            c_send.at[n, 1],
            c_recv.at[n, 1],
            p_cross,
        )
        beside(n, 0)

    for part in range(2):
        f = order[part]
        if part == 0:
            loads[3].wait()
            loads[4].wait()
        picked = mod_ref[ts_ref[f]].astype(jnp.float32)
        shift, scale = picked[0:1], 1.0 + picked[1:2]
        for r in range(rows):
            mix_copy(part, r, t_peer).wait_recv()
            xs = [mixed[f * rows + r, t].astype(jnp.float32) for t in range(n_tp)]
            mean = sum(jnp.sum(x, axis=1, keepdims=True) for x in xs) * (1.0 / width)
            xs = [x - mean for x in xs]
            var = sum(jnp.sum(x * x, axis=1, keepdims=True) for x in xs) * (1.0 / width)
            inv = 1.0 / jnp.sqrt(var + 1e-06)
            for t in range(n_tp):
                at = slice(t * channels, (t + 1) * channels)
                y = xs[t] * inv * scale[:, at] + shift[:, at]
                row = part * half + r * cols
                normed[row : row + cols, at] = y.astype(jnp.bfloat16)
        if part == 0:
            loads[5].wait()
            loads[6].wait()
        at = slice(part * half, (part + 1) * half)
        kv = jnp.dot(normed[at], wkv[...], preferred_element_type=jnp.float32)
        for h in range(local_heads):
            k_at = h * HEAD_DIM
            v_at = local_width + h * HEAD_DIM
            kv_own[h, at] = jnp.concatenate(
                [kv[:, k_at : k_at + HEAD_DIM], kv[:, v_at : v_at + HEAD_DIM]], axis=1
            ).astype(jnp.bfloat16)
        for h in range(heads):
            kv_all[h, 0, at] = kv_own[side * heads + h, at]
        for n, (piece_part, _) in enumerate(pieces):
            if piece_part == part:
                spread_piece(n)

    def relay(n):
        for slot in [k + s for k in far for s in (0, 2)]:
            arrivals[n, slot].wait_recv()
            beside(n, slot)

    loads[7].wait()
    q = jnp.dot(normed[...], wq[...], preferred_element_type=jnp.float32)
    q = q.astype(jnp.bfloat16).astype(jnp.float32) * (HEAD_DIM**-0.5)
    blank = jnp.zeros((tokens, HEAD_DIM), jnp.float32)
    for h in range(local_heads):
        q_h = q[:, h * HEAD_DIM : (h + 1) * HEAD_DIM]
        q_own[h] = jnp.concatenate([q_h, blank], axis=1).astype(jnp.bfloat16)
        q_pack[h] = jnp.concatenate([q_h[:half], q_h[half:]], axis=1).astype(jnp.bfloat16)
    q_copy = go(
        q_pack.at[pl.ds((1 - side) * heads, heads)], q_peer, q_send.at[0], q_recv.at[0], p_pair
    )

    for n in range(len(pieces)):
        relay(n)

    q_copy.wait_recv()
    for slot in [2] + list(range(1, n_patch, 2)):
        arrivals[0, slot].wait_recv()
    o_copies = []
    own = []
    zeros = jnp.zeros((half, HEAD_DIM), jnp.float32)

    def attend(queries, rows_kv):
        scores = lax.dot_general(
            queries, rows_kv, (((1,), (1,)), ((), ())), preferred_element_type=jnp.float32
        )
        exps = jnp.exp(scores - jnp.max(scores, axis=1, keepdims=True))
        totals = jnp.sum(exps, axis=1, keepdims=True)
        summed = jnp.dot(
            exps.astype(jnp.bfloat16), rows_kv, preferred_element_type=jnp.float32
        )
        return summed[:, HEAD_DIM:] / totals

    for h in range(heads):
        for slot in [2] + list(range(1, n_patch, 2)):
            arrivals[h + 1, slot].wait_recv()
        packed = q_peer[h].astype(jnp.float32)
        peer = jnp.concatenate(
            [
                jnp.concatenate([packed[:, :HEAD_DIM], zeros], axis=1),
                jnp.concatenate([packed[:, HEAD_DIM:], zeros], axis=1),
            ],
            axis=0,
        ).astype(jnp.bfloat16)
        mine = q_own[side * heads + h]
        rows_kv = kv_all[h].reshape(n_patch * tokens, 2 * HEAD_DIM)
        last = h == heads - 1
        queries = peer if last else jnp.concatenate([peer, mine], axis=0)
        result = attend(queries, rows_kv)
        o_pack[h] = jnp.concatenate(
            [result[:half], result[half:tokens]], axis=1
        ).astype(jnp.bfloat16)
        o_copies.append(go(o_pack.at[h], o_peer.at[h], o_send.at[h], o_recv.at[h], p_pair))
        own.append(attend(mine, rows_kv) if last else result[tokens:])

    for d in (-1, 1):
        for part in range(2):
            pl.when(p_there[d])(row_copy(d, part).wait_send)
        pl.when(f_there[d])(frame_copy(d).wait_send)
        for g in (-1, 1):
            pl.when(jnp.logical_and(p_there[-g], f_there[d]))(corner_copy(d, g).wait_send)
    for part in range(2):
        for r in range(rows):
            mix_copy(part, r, t_me).wait_send()
    for copy in started:
        copy.wait_send()

    others = []
    for h in range(heads):
        o_copies[h].wait_recv()
        packed = o_peer[h].astype(jnp.float32)
        others.append(jnp.concatenate([packed[:, :HEAD_DIM], packed[:, HEAD_DIM:]], axis=0))
    low = jnp.concatenate(own + others, axis=1)
    high = jnp.concatenate(others + own, axis=1)
    final = jnp.where(side == 0, low, high).astype(jnp.bfloat16)
    for part in range(2):
        piece = final[part * half : (part + 1) * half]
        out_ref[order[part]] = piece.reshape(rows, cols, local_width)


def solution(mesh):
    sizes = tuple(mesh.shape[a] for a in ("frame", "patch", "tp"))
    n_patch = sizes[1]
    far = max(1, n_patch // 4 - 1)

    def local(codes, exps, taps, timestep, modulation, wq, wk, wv):
        frames, rows, cols, channels = codes.shape
        tokens = frames * rows * cols
        width, local_width = wq.shape
        local_heads = local_width // HEAD_DIM
        heads = local_heads // 2
        exps = jnp.transpose(exps, (0, 3, 1, 2))
        bf, f32 = jnp.bfloat16, jnp.float32
        hbm = pl.BlockSpec(memory_space=pltpu.HBM)
        dma = pltpu.SemaphoreType.DMA
        macs = tokens * width * local_width * 3
        macs += 2 * tokens * tokens * n_patch * local_heads * 2 * HEAD_DIM
        return pl.pallas_call(
            functools.partial(kernel, sizes),
            out_shape=jax.ShapeDtypeStruct((frames, rows, cols, local_width), bf),
            in_specs=[hbm] * 8,
            out_specs=pl.BlockSpec(memory_space=pltpu.VMEM),
            scratch_shapes=[
                pltpu.SMEM(timestep.shape, jnp.int32),
                pltpu.VMEM(codes.shape, jnp.int32),
                pltpu.VMEM(exps.shape, jnp.int32),
                pltpu.VMEM(taps.shape, bf),
                pltpu.VMEM(modulation.shape, bf),
                pltpu.VMEM((frames + 2, rows + 2, cols, channels), bf),
                pltpu.VMEM((9, 3, channels), f32),
                pltpu.VMEM((frames * rows, sizes[2], cols, channels), bf),
                pltpu.VMEM((tokens, width), bf),
                pltpu.VMEM((width, 2 * local_width), bf),
                pltpu.VMEM((width, local_width), bf),
                pltpu.VMEM((local_heads, tokens, LANES), bf),
                pltpu.VMEM((heads, n_patch, tokens, LANES), bf),
                pltpu.VMEM((local_heads, tokens, LANES), bf),
                pltpu.VMEM((local_heads, tokens // 2, LANES), bf),
                pltpu.VMEM((heads, tokens // 2, LANES), bf),
                pltpu.VMEM((heads, tokens // 2, LANES), bf),
                pltpu.VMEM((heads, tokens // 2, LANES), bf),
                dma((9,)),
                dma((4,)),
                dma((4,)),
                dma((2,)),
                dma((2,)),
                dma((4,)),
                dma((4,)),
                dma((frames * rows,)),
                dma((frames * rows,)),
                dma((heads + 1,)),
                dma((heads + 1,)),
                dma((heads + 1, 2 * far)),
                dma((heads + 1, 2 * far)),
                dma((heads + 1, n_patch // 2)),
                dma((heads + 1, n_patch // 2)),
                dma((1,)),
                dma((1,)),
                dma((heads,)),
                dma((heads,)),
            ],
            compiler_params=pltpu.CompilerParams(
                collective_id=0, has_side_effects=True, vmem_limit_bytes=56 * 1024 * 1024
            ),
            cost_estimate=pl.CostEstimate(
                flops=2 * macs, bytes_accessed=width * local_width * 6, transcendentals=0
            ),
        )(timestep, codes, exps, taps, modulation, wq, wk, wv)

    in_specs = (
        P("frame", "patch", None, "tp"),
        P("frame", "patch", None, "tp"),
        P(),
        P("frame"),
        P(),
        P(None, "tp"),
        P(None, "tp"),
        P(None, "tp"),
    )
    out_specs = P("frame", "patch", None, "tp")
    return jax.shard_map(local, mesh=mesh, in_specs=in_specs, out_specs=out_specs, check_vma=False)
```

```python
import functools

import jax
import jax.numpy as jnp
from jax import lax
from jax.experimental import pallas as pl
from jax.experimental.pallas import tpu as pltpu
from jax.sharding import PartitionSpec as P

HEAD_DIM = 64
LANES = 128
MESH = pl.DeviceIdType.MESH


def flip(index, mask):
    bit = 1
    while bit <= mask:
        if mask & bit:
            index = index + bit - 2 * bit * lax.rem(lax.div(index, bit), 2)
        bit *= 2
    return index


def kernel(
    sizes,
    ts_hbm,
    codes_hbm,
    exps_hbm,
    taps_hbm,
    mod_hbm,
    wq_hbm,
    wk_hbm,
    wv_hbm,
    out_ref,
    ts_ref,
    codes_ref,
    exps_ref,
    taps_ref,
    mod_ref,
    pad,
    taps,
    mixed,
    normed,
    wkv,
    wq,
    kv_own,
    kv_all,
    q_own,
    q_pack,
    q_peer,
    o_pack,
    o_peer,
    in_sem,
    row_send,
    row_recv,
    frame_send,
    frame_recv,
    corner_send,
    corner_recv,
    mix_send,
    mix_recv,
    a_send,
    a_recv,
    b_send,
    b_recv,
    c_send,
    c_recv,
    q_send,
    q_recv,
    o_send,
    o_recv,
):
    n_frame, n_patch, n_tp = sizes
    frames, rows, cols, channels = codes_ref.shape
    tokens = frames * rows * cols
    half = rows * cols
    local_width = wq_hbm.shape[1]
    local_heads = local_width // HEAD_DIM
    heads = local_heads // 2
    width = n_tp * channels
    f_me = lax.axis_index("frame")
    p_me = lax.axis_index("patch")
    t_me = lax.axis_index("tp")
    t_peer = 1 - t_me
    side = lax.rem(lax.div(p_me, 2), 2)
    lead = lax.rem(f_me, 2)
    order = (lead, 1 - lead)
    p_pair = flip(p_me, 2)
    p_twin = flip(p_me, 1)
    p_cross = flip(p_me, 3)
    far = list(range(4, n_patch, 4))

    loads = [
        pltpu.make_async_copy(src, dst, in_sem.at[i])
        for i, (src, dst) in enumerate(
            [
                (codes_hbm.at[order[1]], codes_ref.at[order[1]]),
                (exps_hbm, exps_ref),
                (taps_hbm, taps_ref),
                (ts_hbm, ts_ref),
                (mod_hbm, mod_ref),
                (wk_hbm, wkv.at[:, pl.ds(0, local_width)]),
                (wv_hbm, wkv.at[:, pl.ds(local_width, local_width)]),
                (wq_hbm, wq),
                (codes_hbm.at[order[0]], codes_ref.at[order[0]]),
            ]
        )
    ]
    for i in (0, 1, 8):
        loads[i].start()

    barrier = pltpu.get_barrier_semaphore()

    def signal(f, p, t):
        pl.semaphore_signal(barrier, inc=1, device_id=(f, p, t), device_id_type=MESH)

    f_there = {-1: f_me > 0, 1: f_me < n_frame - 1}
    p_there = {-1: p_me > 0, 1: p_me < n_patch - 1}
    count = 4 + 2 * len(far)
    for d in (-1, 1):

        @pl.when(f_there[d])
        def _():
            signal(f_me + d, p_me, t_me)

        @pl.when(p_there[d])
        def _():
            signal(f_me, p_me + d, t_me)

        count = count + f_there[d].astype(jnp.int32) + p_there[d].astype(jnp.int32)
    signal(f_me, p_me, t_peer)
    signal(f_me, p_pair, t_me)
    signal(f_me, p_twin, t_me)
    signal(f_me, p_cross, t_me)
    for k in far:
        signal(f_me, flip(p_me, k), t_me)
        signal(f_me, flip(p_me, k + 2), t_me)
    for copy in loads[2:8]:
        copy.start()

    for d in (-1, 1):
        edge_f = 0 if d < 0 else frames + 1
        edge_r = 0 if d < 0 else rows + 1

        @pl.when(jnp.logical_not(f_there[d]))
        def _():
            pad[edge_f] = jnp.zeros((rows + 2, cols, channels), jnp.bfloat16)

        @pl.when(jnp.logical_not(p_there[d]))
        def _():
            pad[1 : 1 + frames, edge_r] = jnp.zeros((frames, cols, channels), jnp.bfloat16)
            for g in (-1, 1):

                @pl.when(f_there[g])
                def _():
                    pad[0 if g < 0 else frames + 1, edge_r] = jnp.zeros(
                        (cols, channels), jnp.bfloat16
                    )

    groups = exps_ref.shape[1]
    span = channels // groups
    spread = (
        lax.broadcasted_iota(jnp.int32, (groups, channels), 1) // span
        == lax.broadcasted_iota(jnp.int32, (groups, channels), 0)
    ).astype(jnp.float32).astype(jnp.bfloat16)
    loads[1].wait()

    def dequantize(f):
        for r in range(rows):
            factor = jnp.left_shift(jnp.ones((groups, cols), jnp.int32), exps_ref[f, :, r, :] + 8)
            factor = (factor.astype(jnp.float32) * (2.0**-8)).astype(jnp.bfloat16)
            factor = lax.dot_general(
                factor, spread, (((0,), (0,)), ((), ())), preferred_element_type=jnp.float32
            )
            values = codes_ref[f, r].astype(jnp.float32) * factor
            pad[f + 1, r + 1] = values.astype(jnp.bfloat16)

    def row_copy(d, part):
        frame = 1 + order[1 - part]
        number = (0 if d < 0 else 2) + part
        return pltpu.make_async_remote_copy(
            src_ref=pad.at[frame, rows if d > 0 else 1],
            dst_ref=pad.at[frame, 0 if d > 0 else rows + 1],
            send_sem=row_send.at[number],
            recv_sem=row_recv.at[number],
            device_id=(f_me, p_me + d, t_me),
            device_id_type=MESH,
        )

    def frame_copy(d):
        number = 0 if d < 0 else 1
        return pltpu.make_async_remote_copy(
            src_ref=pad.at[frames if d > 0 else 1, pl.ds(1, rows)],
            dst_ref=pad.at[0 if d > 0 else frames + 1, pl.ds(1, rows)],
            send_sem=frame_send.at[number],
            recv_sem=frame_recv.at[number],
            device_id=(f_me + d, p_me, t_me),
            device_id_type=MESH,
        )

    def corner_copy(d, g):
        number = (0 if d < 0 else 2) + (0 if g < 0 else 1)
        row = 0 if g > 0 else rows + 1
        return pltpu.make_async_remote_copy(
            src_ref=pad.at[frames if d > 0 else 1, row],
            dst_ref=pad.at[0 if d > 0 else frames + 1, row],
            send_sem=corner_send.at[number],
            recv_sem=corner_recv.at[number],
            device_id=(f_me + d, p_me, t_me),
            device_id_type=MESH,
        )

    for part in range(2):
        loads[0 if part == 0 else 8].wait()
        dequantize(order[1 - part])
        if part == 0:
            pl.semaphore_wait(barrier, count)
        for d in (-1, 1):
            pl.when(p_there[d])(row_copy(d, part).start)
    for d in (-1, 1):
        pl.when(f_there[d])(frame_copy(d).start)

    loads[2].wait()
    own_lanes = pl.ds(pl.multiple_of(t_me * channels, LANES), channels)
    for a in range(3):
        for b in range(3):
            taps[a * 3 + b] = taps_ref[a, b, :, own_lanes].astype(jnp.float32)

    for part in range(2):
        for g in (-1, 1):
            pl.when(p_there[-g])(row_copy(g, part).wait_recv)
            for d in (-1, 1):
                first = (lead == 1) if d < 0 else (lead == 0)
                mine = first if part == 0 else jnp.logical_not(first)
                ready = jnp.logical_and(jnp.logical_and(p_there[-g], f_there[d]), mine)
                pl.when(ready)(corner_copy(d, g).start)
    for d in (-1, 1):
        pl.when(f_there[-d])(frame_copy(d).wait_recv)

    col = lax.broadcasted_iota(jnp.int32, (cols, LANES), 0)

    def mix_copy(part, r, t):
        i = order[part] * rows + r
        return pltpu.make_async_remote_copy(
            src_ref=mixed.at[i, t],
            dst_ref=mixed.at[i, t],
            send_sem=mix_send.at[part * rows + r],
            recv_sem=mix_recv.at[part * rows + r],
            device_id=(f_me, p_me, t_peer),
            device_id_type=MESH,
        )

    for part in range(2):
        f = order[part]
        for d in (-1, 1):
            for g in (-1, 1):
                needs = (f == 0) if d > 0 else (f == frames - 1)
                ready = jnp.logical_and(jnp.logical_and(p_there[-g], f_there[-d]), needs)
                pl.when(ready)(corner_copy(d, g).wait_recv)
        for r in range(rows):

            def conv(step, carry):
                at = pl.ds(pl.multiple_of(step * LANES, LANES), LANES)
                sums = [jnp.zeros((cols, LANES), jnp.float32) for _ in range(3)]
                centre = None
                for a in range(3):
                    for b in range(3):
                        x = pad[f + a, r + b, :, at].astype(jnp.float32)
                        if a == 1 and b == 1:
                            centre = x
                        w = taps[a * 3 + b, :, at]
                        for c in range(3):
                            sums[c] = sums[c] + x * w[c : c + 1]
                before = jnp.where(col == 0, 0.0, pltpu.roll(sums[0], 1, 0))
                after = jnp.where(col == cols - 1, 0.0, pltpu.roll(sums[2], cols - 1, 0))
                total = centre + (sums[1] + (before + after))
                mixed[f * rows + r, t_me, :, at] = total.astype(jnp.bfloat16)
                return carry

            lax.fori_loop(0, channels // LANES, conv, 0)
            mix_copy(part, r, t_me).start()

    started = []

    def go(src, dst, s_sem, r_sem, p):
        copy = pltpu.make_async_remote_copy(
            src_ref=src,
            dst_ref=dst,
            send_sem=s_sem,
            recv_sem=r_sem,
            device_id=(f_me, p, t_me),
            device_id_type=MESH,
        )
        copy.start()
        started.append(copy)
        return copy

    pieces = [(0, pl.ds(0, heads))] + [(1, pl.ds(h, 1)) for h in range(heads)]
    arrivals = {}

    def beside(n, slot):
        part, hs = pieces[n]
        at = pl.ds(part * half, half)
        arrivals[n, slot + 1] = go(
            kv_all.at[hs, slot, at],
            kv_all.at[hs, slot + 1, at],
            c_send.at[n, slot // 2],
            c_recv.at[n, slot // 2],
            p_twin,
        )

    def spread_piece(n):
        part, hs = pieces[n]
        at = pl.ds(part * half, half)
        size = heads if part == 0 else 1
        first = 0 if part == 0 else n - 1
        mine = pl.ds(side * heads + first, size)
        other = pl.ds((1 - side) * heads + first, size)
        for m, k in enumerate(far):
            for slot, src in ((0, mine), (2, other)):
                arrivals[n, k + slot] = go(
                    kv_own.at[src, at],
                    kv_all.at[hs, k + slot, at],
                    b_send.at[n, 2 * m + slot // 2],
                    b_recv.at[n, 2 * m + slot // 2],
                    flip(p_me, k + slot),
                )
        arrivals[n, 2] = go(
            kv_own.at[other, at], kv_all.at[hs, 2, at], a_send.at[n], a_recv.at[n], p_pair
        )
        arrivals[n, 3] = go(
            kv_own.at[other, at],
            kv_all.at[hs, 3, at],
            c_send.at[n, 1],
            c_recv.at[n, 1],
            p_cross,
        )
        beside(n, 0)

    for part in range(2):
        f = order[part]
        if part == 0:
            loads[3].wait()
            loads[4].wait()
        picked = mod_ref[ts_ref[f]].astype(jnp.float32)
        shift, scale = picked[0:1], 1.0 + picked[1:2]
        for r in range(rows):
            mix_copy(part, r, t_peer).wait_recv()
            xs = [mixed[f * rows + r, t].astype(jnp.float32) for t in range(n_tp)]
            mean = sum(jnp.sum(x, axis=1, keepdims=True) for x in xs) * (1.0 / width)
            xs = [x - mean for x in xs]
            var = sum(jnp.sum(x * x, axis=1, keepdims=True) for x in xs) * (1.0 / width)
            inv = 1.0 / jnp.sqrt(var + 1e-06)
            for t in range(n_tp):
                at = slice(t * channels, (t + 1) * channels)
                y = xs[t] * inv * scale[:, at] + shift[:, at]
                row = part * half + r * cols
                normed[row : row + cols, at] = y.astype(jnp.bfloat16)
        if part == 0:
            loads[5].wait()
            loads[6].wait()
        at = slice(part * half, (part + 1) * half)
        kv = jnp.dot(normed[at], wkv[...], preferred_element_type=jnp.float32)
        for h in range(local_heads):
            k_at = h * HEAD_DIM
            v_at = local_width + h * HEAD_DIM
            kv_own[h, at] = jnp.concatenate(
                [kv[:, k_at : k_at + HEAD_DIM], kv[:, v_at : v_at + HEAD_DIM]], axis=1
            ).astype(jnp.bfloat16)
        for h in range(heads):
            kv_all[h, 0, at] = kv_own[side * heads + h, at]
        for n, (piece_part, _) in enumerate(pieces):
            if piece_part == part:
                spread_piece(n)

    def relay(n):
        for slot in [k + s for k in far for s in (0, 2)]:
            arrivals[n, slot].wait_recv()
            beside(n, slot)

    loads[7].wait()
    q = jnp.dot(normed[...], wq[...], preferred_element_type=jnp.float32)
    q = q.astype(jnp.bfloat16).astype(jnp.float32) * (HEAD_DIM**-0.5)
    blank = jnp.zeros((tokens, HEAD_DIM), jnp.float32)
    for h in range(local_heads):
        q_h = q[:, h * HEAD_DIM : (h + 1) * HEAD_DIM]
        q_own[h] = jnp.concatenate([q_h, blank], axis=1).astype(jnp.bfloat16)
        q_pack[h] = jnp.concatenate([q_h[:half], q_h[half:]], axis=1).astype(jnp.bfloat16)
    q_copy = go(
        q_pack.at[pl.ds((1 - side) * heads, heads)], q_peer, q_send.at[0], q_recv.at[0], p_pair
    )

    for n in range(len(pieces)):
        relay(n)

    q_copy.wait_recv()
    for slot in [2] + list(range(1, n_patch, 2)):
        arrivals[0, slot].wait_recv()
    o_copies = []
    own = []
    zeros = jnp.zeros((half, HEAD_DIM), jnp.float32)

    def attend(queries, rows_kv):
        scores = lax.dot_general(
            queries, rows_kv, (((1,), (1,)), ((), ())), preferred_element_type=jnp.float32
        )
        exps = jnp.exp(scores - jnp.max(scores, axis=1, keepdims=True))
        totals = jnp.sum(exps, axis=1, keepdims=True)
        summed = jnp.dot(
            exps.astype(jnp.bfloat16), rows_kv, preferred_element_type=jnp.float32
        )
        return summed[:, HEAD_DIM:] / totals

    for h in range(heads):
        for slot in [2] + list(range(1, n_patch, 2)):
            arrivals[h + 1, slot].wait_recv()
        packed = q_peer[h].astype(jnp.float32)
        peer = jnp.concatenate(
            [
                jnp.concatenate([packed[:, :HEAD_DIM], zeros], axis=1),
                jnp.concatenate([packed[:, HEAD_DIM:], zeros], axis=1),
            ],
            axis=0,
        ).astype(jnp.bfloat16)
        mine = q_own[side * heads + h]
        rows_kv = kv_all[h].reshape(n_patch * tokens, 2 * HEAD_DIM)
        last = h == heads - 1
        queries = peer if last else jnp.concatenate([peer, mine], axis=0)
        result = attend(queries, rows_kv)
        o_pack[h] = jnp.concatenate(
            [result[:half], result[half:tokens]], axis=1
        ).astype(jnp.bfloat16)
        o_copies.append(go(o_pack.at[h], o_peer.at[h], o_send.at[h], o_recv.at[h], p_pair))
        own.append(attend(mine, rows_kv) if last else result[tokens:])

    for d in (-1, 1):
        for part in range(2):
            pl.when(p_there[d])(row_copy(d, part).wait_send)
        pl.when(f_there[d])(frame_copy(d).wait_send)
        for g in (-1, 1):
            pl.when(jnp.logical_and(p_there[-g], f_there[d]))(corner_copy(d, g).wait_send)
    for part in range(2):
        for r in range(rows):
            mix_copy(part, r, t_me).wait_send()
    for copy in started:
        copy.wait_send()

    others = []
    for h in range(heads):
        o_copies[h].wait_recv()
        packed = o_peer[h].astype(jnp.float32)
        others.append(jnp.concatenate([packed[:, :HEAD_DIM], packed[:, HEAD_DIM:]], axis=0))
    low = jnp.concatenate(own + others, axis=1)
    high = jnp.concatenate(others + own, axis=1)
    final = jnp.where(side == 0, low, high).astype(jnp.bfloat16)
    for part in range(2):
        piece = final[part * half : (part + 1) * half]
        out_ref[order[part]] = piece.reshape(rows, cols, local_width)


def solution(mesh):
    sizes = tuple(mesh.shape[a] for a in ("frame", "patch", "tp"))
    n_patch = sizes[1]
    far = max(1, n_patch // 4 - 1)

    def local(codes, exps, taps, timestep, modulation, wq, wk, wv):
        frames, rows, cols, channels = codes.shape
        tokens = frames * rows * cols
        width, local_width = wq.shape
        local_heads = local_width // HEAD_DIM
        heads = local_heads // 2
        exps = jnp.transpose(exps, (0, 3, 1, 2))
        bf, f32 = jnp.bfloat16, jnp.float32
        hbm = pl.BlockSpec(memory_space=pltpu.HBM)
        dma = pltpu.SemaphoreType.DMA
        macs = tokens * width * local_width * 3
        macs += 2 * tokens * tokens * n_patch * local_heads * 2 * HEAD_DIM
        return pl.pallas_call(
            functools.partial(kernel, sizes),
            out_shape=jax.ShapeDtypeStruct((frames, rows, cols, local_width), bf),
            in_specs=[hbm] * 8,
            out_specs=pl.BlockSpec(memory_space=pltpu.VMEM),
            scratch_shapes=[
                pltpu.SMEM(timestep.shape, jnp.int32),
                pltpu.VMEM(codes.shape, jnp.int32),
                pltpu.VMEM(exps.shape, jnp.int32),
                pltpu.VMEM(taps.shape, bf),
                pltpu.VMEM(modulation.shape, bf),
                pltpu.VMEM((frames + 2, rows + 2, cols, channels), bf),
                pltpu.VMEM((9, 3, channels), f32),
                pltpu.VMEM((frames * rows, sizes[2], cols, channels), bf),
                pltpu.VMEM((tokens, width), bf),
                pltpu.VMEM((width, 2 * local_width), bf),
                pltpu.VMEM((width, local_width), bf),
                pltpu.VMEM((local_heads, tokens, LANES), bf),
                pltpu.VMEM((heads, n_patch, tokens, LANES), bf),
                pltpu.VMEM((local_heads, tokens, LANES), bf),
                pltpu.VMEM((local_heads, tokens // 2, LANES), bf),
                pltpu.VMEM((heads, tokens // 2, LANES), bf),
                pltpu.VMEM((heads, tokens // 2, LANES), bf),
                pltpu.VMEM((heads, tokens // 2, LANES), bf),
                dma((9,)),
                dma((4,)),
                dma((4,)),
                dma((2,)),
                dma((2,)),
                dma((4,)),
                dma((4,)),
                dma((frames * rows,)),
                dma((frames * rows,)),
                dma((heads + 1,)),
                dma((heads + 1,)),
                dma((heads + 1, 2 * far)),
                dma((heads + 1, 2 * far)),
                dma((heads + 1, n_patch // 2)),
                dma((heads + 1, n_patch // 2)),
                dma((1,)),
                dma((1,)),
                dma((heads,)),
                dma((heads,)),
            ],
            compiler_params=pltpu.CompilerParams(
                collective_id=0, has_side_effects=True, vmem_limit_bytes=55040 * 1024
            ),
            cost_estimate=pl.CostEstimate(
                flops=2 * macs, bytes_accessed=width * local_width * 6, transcendentals=0
            ),
        )(timestep, codes, exps, taps, modulation, wq, wk, wv)

    in_specs = (
        P("frame", "patch", None, "tp"),
        P("frame", "patch", None, "tp"),
        P(),
        P("frame"),
        P(),
        P(None, "tp"),
        P(None, "tp"),
        P(None, "tp"),
    )
    out_specs = P("frame", "patch", None, "tp")
    return jax.shard_map(local, mesh=mesh, in_specs=in_specs, out_specs=out_specs, check_vma=False)
```
